512 devices in a mesh: cols: 16 (over y, x), depth: 32 (over z, core).
Axes of the slice: x: 4, y: 4, z: 16, core: 2. Of those that a mesh axis runs over, the one named last changes fastest.
Arguments:
- mass_concentration: bfloat16 [1024, 128, 2048], P('depth', None, 'cols'), may hold values from 0.25 to 2
- thermal_field: bfloat16 [1024, 128, 2048], P('depth', None, 'cols'), may hold values from 0.5 to 2.5
- absorption_coefficient: bfloat16 [256], replicated, may hold values from 4.863739e-05 to 0.0048828125
- glow_palette: bfloat16 [3, 256], replicated, may hold values from 0.19921875 to 1
- integer_skew_steps: int32 [2, 1024], replicated, may hold values from -8 to 8, as said below
- subcell_remainder: float32 [2, 1024], replicated, may hold values from 0 to 1
Outputs:
- image_frame: float32 [4, 128, 2048], P(None, 'depth', 'cols')
The draws below stay inside these ranges and needn't reach their ends.
Inputs may be any that keep to these rules, and one draw needn't show every extreme that they name: `integer_skew_steps`: row 0 shifts along columns, row 1 along rows; each row holds both -8 and 8.
All inputs are finite; a program needn't handle non-finite values.
Results may differ from the reference program's by a relative error of at most 0.00055.
Values may be sent and summed in bfloat16 or wider, within the bound.
A program may use at most 128 MiB of HBM per device.

```python
import math
import jax
import jax.numpy as jnp
from jax import lax

PICTURE_HEIGHT = 128
SZ = 32
TRANSFER_CLASSES = 256
SH = 8
PICTURE_WIDTHS = 2048
DEPTH_LAYERS = 1024
SLABS = 32


def draw_integer_skew_steps(key, part):
    values = jax.random.randint(key, (2, DEPTH_LAYERS), -SH, SH + 1, dtype=jnp.int32)
    low_spots = jax.random.randint(jax.random.fold_in(key, 11), (2,), 0, DEPTH_LAYERS // 2, dtype=jnp.int32)
    high_spots = jax.random.randint(jax.random.fold_in(key, 13), (2,), DEPTH_LAYERS // 2, DEPTH_LAYERS, dtype=jnp.int32)
    row_pick = jnp.arange(2, dtype=jnp.int32)
    values = values.at[row_pick, low_spots].set(-SH)
    values = values.at[row_pick, high_spots].set(SH)
    return values.astype(jnp.int32)


def block_levels(rng, dims, cuts, smallest, largest):
    loudness = 1.0
    for dim, blocks in cuts:
        heights = jax.random.uniform(jax.random.fold_in(jax.random.fold_in(rng, 6), dim), (blocks,), jnp.float32, smallest / len(cuts), largest / len(cuts))
        loudness = loudness * jnp.repeat(jnp.exp(heights), dims[dim] // blocks).reshape((-1,) + (1,) * (len(dims) - 1 - dim))
    return loudness


def setup_inputs(seed: int = 0) -> dict:
    splits = jax.random.split(jax.random.key(seed), 7)
    mass_concentration = jnp.clip(jnp.exp(math.log(2.0) - 2.0794415 * jax.random.uniform(splits[0], (DEPTH_LAYERS, PICTURE_HEIGHT, PICTURE_WIDTHS), jnp.float32) ** block_levels(splits[0], (DEPTH_LAYERS, PICTURE_HEIGHT, PICTURE_WIDTHS), ((0, 32), (2, 16)), -0.2, 0.2)), 0.25, 2.0).astype(jnp.bfloat16)
    thermal_field = jnp.clip(jnp.exp(math.log(2.5) - 1.609438 * jax.random.uniform(splits[1], (DEPTH_LAYERS, PICTURE_HEIGHT, PICTURE_WIDTHS), jnp.float32) ** block_levels(splits[1], (DEPTH_LAYERS, PICTURE_HEIGHT, PICTURE_WIDTHS), ((0, 32), (2, 16)), -0.2, 0.2)), 0.5, 2.5).astype(jnp.bfloat16)
    absorption_coefficient = jnp.clip(jnp.exp(jax.random.uniform(splits[2], (TRANSFER_CLASSES,), jnp.float32, math.log(4.863739013671875e-05), math.log(0.0048828125))), 4.863739013671875e-05, 0.0048828125).astype(jnp.bfloat16)
    glow_palette = jnp.clip(jax.random.uniform(splits[3], (3, TRANSFER_CLASSES), jnp.float32, 0.19921875, 1.0), 0.19921875, 1.0).astype(jnp.bfloat16)
    integer_skew_steps = draw_integer_skew_steps(jax.random.fold_in(splits[6], 71), 0)
    subcell_remainder = jnp.clip(jax.random.uniform(splits[5], (2, DEPTH_LAYERS), jnp.float32, 0.0, 1.0), 0.0, 1.0)
    return dict(mass_concentration=mass_concentration, thermal_field=thermal_field, absorption_coefficient=absorption_coefficient, glow_palette=glow_palette, integer_skew_steps=integer_skew_steps, subcell_remainder=subcell_remainder)


light_x = 0.48
light_y = 0.6
light_z = 0.64
ambient = 0.3
diffuse = 0.7
softening = 0.25


def shading_of(window):
    grad_x = (window[1, 1:-1, 2:] - window[1, 1:-1, :-2]) * 0.5
    grad_y = (window[1, 2:, 1:-1] - window[1, :-2, 1:-1]) * 0.5
    grad_z = (window[2, 1:-1, 1:-1] - window[0, 1:-1, 1:-1]) * 0.5
    facing = light_x * grad_x + light_y * grad_y + light_z * grad_z
    length = grad_x * grad_x + grad_y * grad_y + grad_z * grad_z + softening
    return ambient + diffuse * facing * facing / length


def two_weights(fraction_now):
    keep_weight = lax.optimization_barrier((1.0 - fraction_now).astype(jnp.bfloat16)).astype(jnp.float32)
    next_weight = lax.optimization_barrier(fraction_now.astype(jnp.bfloat16)).astype(jnp.float32)
    return keep_weight, next_weight


def reference(mass_concentration, thermal_field, absorption_coefficient, glow_palette, integer_skew_steps, subcell_remainder):
    rim_width = SH + 1
    dens_pad = jnp.pad(mass_concentration, 1)
    backward = integer_skew_steps[0, 0] > 0

    def slice_sample(layer_iterate):
        window = lax.dynamic_slice_in_dim(dens_pad, layer_iterate, 3, 0).astype(jnp.float32)
        lighting_factor = shading_of(window)
        cell_heat_reading = thermal_field[layer_iterate].astype(jnp.float32)
        classes_present = jnp.clip(jnp.floor((cell_heat_reading - 0.5) * (TRANSFER_CLASSES // 2)), 0, TRANSFER_CLASSES - 1).astype(jnp.int32)
        extinction = absorption_coefficient[classes_present].astype(jnp.float32)
        radiance_triples = glow_palette[:, classes_present].astype(jnp.float32)
        alpha_coverage = 1.0 - jnp.exp(-extinction * window[1, 1:-1, 1:-1])
        grid_element = jnp.concatenate([alpha_coverage * lighting_factor * cell_heat_reading * radiance_triples, alpha_coverage[None]], 0)
        grid_element = lax.optimization_barrier(grid_element.astype(jnp.bfloat16)).astype(jnp.float32)
        wide_pad = jnp.pad(grid_element, ((0, 0), (0, 0), (rim_width, rim_width)))
        keep_weight, next_weight = two_weights(subcell_remainder[0, layer_iterate])
        offset = integer_skew_steps[0, layer_iterate].astype(jnp.int32)
        sheared = (lax.dynamic_slice_in_dim(wide_pad, rim_width + offset, PICTURE_WIDTHS, 2) * keep_weight
                   + lax.dynamic_slice_in_dim(wide_pad, rim_width + offset + 1, PICTURE_WIDTHS, 2) * next_weight)
        sheared = lax.optimization_barrier(sheared.astype(jnp.bfloat16)).astype(jnp.float32)
        tall_pad = jnp.pad(sheared, ((0, 0), (rim_width, rim_width), (0, 0)))
        keep_row, next_row = two_weights(subcell_remainder[1, layer_iterate])
        offset_row = integer_skew_steps[1, layer_iterate].astype(jnp.int32)
        return (lax.dynamic_slice_in_dim(tall_pad, rim_width + offset_row, PICTURE_HEIGHT, 1) * keep_row
                + lax.dynamic_slice_in_dim(tall_pad, rim_width + offset_row + 1, PICTURE_HEIGHT, 1) * next_row)

    def slab_partial(slab_number):
        def advance(carry, probe_location):
            color_sum, transmit = carry
            local_values = jnp.where(backward, SZ - 1 - probe_location, probe_location).astype(jnp.int32)
            sample = slice_sample(slab_number * SZ + local_values)
            return (color_sum + transmit * sample[:3], transmit * (1.0 - sample[3])), None

        initial = (jnp.zeros((3, PICTURE_HEIGHT, PICTURE_WIDTHS), jnp.float32), jnp.ones((PICTURE_HEIGHT, PICTURE_WIDTHS), jnp.float32))
        result, _ = lax.scan(advance, initial, jnp.arange(SZ, dtype=jnp.int32))
        return result

    color_sums, transmits = lax.map(slab_partial, jnp.arange(SLABS, dtype=jnp.int32))
    slab_numbers = jnp.arange(SLABS, dtype=jnp.int32)
    ranks = jnp.where(backward, SLABS - 1 - slab_numbers, slab_numbers).astype(jnp.int32)

    def before_of(slab_number):
        earlier = ranks < ranks[slab_number]
        return jnp.prod(jnp.where(earlier[:, None, None], transmits, 1.0), axis=0)

    before = lax.map(before_of, slab_numbers)
    radiance_triples = jnp.sum(before[:, None] * color_sums, axis=0)
    coverage = jnp.sum(before * (1.0 - transmits), axis=0)
    return jnp.concatenate([radiance_triples, coverage[None]], 0)
```

```python
import functools
import math

import jax
import jax.numpy as jnp
from jax import lax
from jax.experimental import pallas as pl
from jax.experimental.pallas import tpu as pltpu
from jax.sharding import PartitionSpec as P

MESH = pl.DeviceIdType.MESH
BF = jnp.bfloat16
F32 = jnp.float32
I32 = jnp.int32
LANES = 128
PAD = 8
GROUP = 4
SLOT = 16
SLOTS = 8
LEFT = 12
RIGHT = 4

ROOT = math.sqrt(0.7) * 2.0 ** -5
KX, KY, KZ = 0.48 * ROOT, 0.6 * ROOT, 0.64 * ROOT
AMBIENT = 0.3 * 2.0 ** -10
MAGIC0 = 1.5 * 2.0 ** 33
MAGIC1 = 1.5 * 2.0 ** 35
BIAS = 10240.0 * 1024.0
EXPO = -(2.0 ** -32) * math.log2(math.e)


def iota(shape, dim):
    return lax.broadcasted_iota(I32, shape, dim)


def table_words(absorption, glow):
    a = absorption.astype(F32) * 2.0 ** 22
    g = glow.astype(F32) * 2.0 ** 10
    w0 = (a - 10240.0) * 1024.0 + (g[0] - 612.0)
    w1 = g[1] * 4096.0 + g[2]
    words = jnp.concatenate([w0.reshape(2, LANES), w1.reshape(2, LANES)], 0)
    return jnp.broadcast_to(words[:, None, :], (4, 8, LANES))


def round_bf(x):
    return x.astype(BF).astype(F32)


def classify(d, up, down, zm, zp, gx, t, words):
    gy = down - up
    gz = zp - zm
    f = KX * gx + KY * gy + KZ * gz
    length = gx * gx + gy * gy + gz * gz + 1.0
    shade = AMBIENT + f * f / length
    index = jnp.clip((t * 128.0 - 64.0).astype(I32), 0, 255)
    high = index >= LANES
    low_bits = index & (LANES - 1)

    def pick(word):
        table = jnp.concatenate([word] * (index.shape[0] // 8), 0)
        return jnp.take_along_axis(table, low_bits, axis=1, mode="promise_in_bounds")

    w0 = jnp.where(high, pick(words[1]), pick(words[0]))
    w1 = jnp.where(high, pick(words[3]), pick(words[2]))
    a = (w0 + MAGIC0) - (MAGIC0 - BIAS)
    g0 = (w0 - a) + (612.0 + BIAS)
    g1 = (w1 + MAGIC1) - MAGIC1
    g2 = w1 - g1
    alpha = 1.0 - jnp.exp2(a * (d * EXPO))
    p = alpha * shade * t
    return p * g0, (p * 2.0 ** -12) * g1, p * g2, alpha


def kernel(
    skew, frac, words_ref, dens, temp, out,
    dv, tv, df, diag,
    pd12, pd4, pt12, pt4, rd12, rd4, rt12, rt4,
    lf, rf, sd, dh, zph, zmh, th,
    gx_ref, vx, vh, sel, grad, wall, sheared, carry,
    hbuf, hrecv, comb, frecv,
    local_sem, plane_send, plane_recv, pack_send, pack_recv, pair_send, pair_recv,
    out_send, out_recv,
):
    depth, rows, _ = tv.shape
    chips = comb.shape[0]
    col, dep = lax.axis_index("cols"), lax.axis_index("depth")
    ncol, ndep = lax.axis_size("cols"), lax.axis_size("depth")
    chip, core = dep // 2, dep % 2
    left, right = lax.rem(col + ncol - 1, ncol), lax.rem(col + 1, ncol)
    lower, upper = lax.rem(dep + ndep - 1, ndep), lax.rem(dep + 1, ndep)
    pair = dep + 1 - 2 * core
    base = dep * depth

    barrier = pltpu.get_barrier_semaphore()
    for c in (left, col, right):
        for e in (lower, dep, upper):
            if c is col and e is dep:
                continue
            pl.semaphore_signal(barrier, inc=1, device_id=(c, e), device_id_type=MESH)

    def greet(o, _):
        other = lax.rem(chip + o, chips) * 2 + core
        pl.semaphore_signal(barrier, inc=1, device_id=(col, other), device_id_type=MESH)
        return 0

    lax.fori_loop(1, chips, greet, 0)

    dens_in = pltpu.make_async_copy(dens, dv.at[pl.ds(1, depth)], local_sem.at[0])
    temp_in = pltpu.make_async_copy(temp, tv, local_sem.at[1])
    dens_in.start()
    temp_in.start()

    lane = iota((8, LANES), 1)
    kk, slot = lane % SLOT, lane // SLOT
    src = iota((LANES, 2 * LANES), 0)
    dst = iota((LANES, 2 * LANES), 1)
    move = jnp.where(dst < LANES, LEFT, RIGHT)
    off = (src + move) % LANES

    def build_sel(j, _):
        hit = (off < SLOT) & (off + j * SLOT == dst % LANES)
        sel[pl.ds(pl.multiple_of(j * LANES, LANES), LANES), :] = jnp.where(hit, 1.0, 0.0).astype(BF)
        return 0

    lax.fori_loop(0, SLOTS, build_sel, 0)
    gk, gc = iota((LANES, LANES), 0), iota((LANES, LANES), 1)
    grad[...] = (
        jnp.where(gk == gc + 1, 1.0, 0.0) - jnp.where(gk == gc - 1, 1.0, 0.0)
    ).astype(BF)
    def weights(row, z):
        part = jnp.full((8, LANES), frac[row, base + z], F32)
        return (1.0 - part).astype(BF).astype(F32), part.astype(BF).astype(F32)

    gap = jnp.where((gk > 0) & (gk < LANES - 1), gk - gc, 1000)
    hk, hc = iota((SLOT, LANES), 0), iota((SLOT, LANES), 1)

    def build_weights(z, _):
        s = skew[0, base + z]
        a0, a1 = weights(0, z)
        a0, a1 = a0[0:1], a1[0:1]
        wall[z, 0:LANES, :] = jnp.where(gap == s, a0, jnp.where(gap == s + 1, a1, 0.0)).astype(BF)
        wall[z, LANES:, :] = jnp.zeros((LANES, LANES), BF)
        use_right = (s >= 1) | ((s >= -1) & (hk < SLOT // 2))
        hcol = jnp.where(use_right, hk + (LANES - RIGHT), hk - LEFT)
        valid = (hcol <= 0) | (hcol >= LANES - 1)
        hgap = jnp.where(valid, hcol - hc, 1000)
        at = pl.ds(pl.multiple_of(LANES + (z // GROUP) * SLOT, SLOT), SLOT)
        wall[z, at, :] = jnp.where(hgap == s, a0, jnp.where(hgap == s + 1, a1, 0.0)).astype(BF)
        return 0

    lax.fori_loop(0, depth, build_weights, 0)

    def zero_df(z, _):
        df[z, 0:PAD, :] = jnp.zeros((PAD, LANES), F32)
        df[z, PAD + rows : PAD + rows + 8, :] = jnp.zeros((8, LANES), F32)
        return 0

    lax.fori_loop(0, depth + 2, zero_df, 0)

    def zero_sheared(k, _):
        for s in range(2):
            for c in range(4):
                sheared[s, k, c, 0:PAD, :] = jnp.zeros((PAD, LANES), F32)
                sheared[s, k, c, PAD + rows : PAD + rows + 16, :] = jnp.zeros((16, LANES), F32)
        dh[k, 0:PAD, :] = jnp.zeros((PAD, LANES), F32)
        dh[k, PAD + rows : PAD + rows + 8, :] = jnp.zeros((8, LANES), F32)
        return 0

    lax.fori_loop(0, GROUP, zero_sheared, 0)

    pl.semaphore_wait(barrier, 8 + chips - 1)

    planes = []
    for n, (e, plane, end) in enumerate(((upper, depth - 1, 0), (lower, 0, 1))):
        for m, c in enumerate((col, right, left)):
            target = dv.at[end * (depth + 1)] if m == 0 else diag.at[end, m - 1]
            planes.append(
                pltpu.make_async_remote_copy(
                    src_ref=dens.at[plane], dst_ref=target,
                    send_sem=plane_send.at[n, m], recv_sem=plane_recv.at[n, m],
                    device_id=(c, e), device_id_type=MESH,
                )
            )
    for copy in planes:
        copy.start()

    def pack(source, first, p12, p4):
        def step(i, _):
            lhs = jnp.concatenate([source[first + GROUP * j + i] for j in range(SLOTS)], 1)
            both = jnp.dot(lhs, sel[...], preferred_element_type=F32).astype(BF)
            p12[i] = both[:, :LANES]
            p4[i] = both[:, LANES:]
            return 0

        lax.fori_loop(0, GROUP, step, 0)

    def send_pack(n, p, r, c):
        copy = pltpu.make_async_remote_copy(
            src_ref=p, dst_ref=r, send_sem=pack_send.at[n], recv_sem=pack_recv.at[n],
            device_id=(c, dep), device_id_type=MESH,
        )
        copy.start()
        return copy

    dens_in.wait()
    pack(dv, 1, pd12, pd4)
    packs = [send_pack(0, pd12, rd12, right), send_pack(1, pd4, rd4, left)]
    temp_in.wait()
    pack(tv, 0, pt12, pt4)
    packs += [send_pack(2, pt12, rt12, right), send_pack(3, pt4, rt4, left)]

    def widen(z, _):
        df[z, PAD : PAD + rows, :] = dv[z].astype(F32)
        return 0

    lax.fori_loop(1, depth + 1, widen, 0)
    for copy in planes:
        copy.wait_recv()
    df[0, PAD : PAD + rows, :] = jnp.where(dep > 0, dv[0].astype(F32), 0.0)
    df[depth + 1, PAD : PAD + rows, :] = jnp.where(dep < ndep - 1, dv[depth + 1].astype(F32), 0.0)
    words = [words_ref[k] for k in range(4)]

    def main_step(z, _):
        gx_ref[...] = jnp.dot(dv[z + 1], grad[...], preferred_element_type=F32)
        for r in range(0, rows, 16):
            q = PAD + r
            values = classify(
                df[z + 1, q : q + 16, :], df[z + 1, q - 1 : q + 15, :], df[z + 1, q + 1 : q + 17, :],
                df[z, q : q + 16, :], df[z + 2, q : q + 16, :],
                gx_ref[r : r + 16, :], tv[z, r : r + 16, :].astype(F32), words,
            )
            for c in range(4):
                vx[z, c, r : r + 16, :] = values[c].astype(BF)
        return 0

    lax.fori_loop(0, depth, main_step, 0)

    for copy in packs:
        copy.wait_recv()
    kk16, slot16 = kk[0:1], slot[0:1]
    has_left, has_right = col > 0, col < ncol - 1

    def windows(i, _):
        l = jnp.where(kk16 < LEFT, jnp.where(has_left, rd12[i].astype(F32), 0.0), pd12[i].astype(F32))
        r = jnp.where(kk16 < RIGHT, pd4[i].astype(F32), jnp.where(has_right, rd4[i].astype(F32), 0.0))
        lf[i + 1] = l
        rf[i + 1] = r
        return 0

    lax.fori_loop(0, GROUP, windows, 0)
    for end, j, tile, other, shift, has in (
        (0, 0, 0, GROUP, SLOT, dep > 0),
        (1, SLOTS - 1, GROUP + 1, 1, LANES - SLOT, dep < ndep - 1),
    ):
        own = df[end * (depth + 1), PAD : PAD + rows, :]
        dl = jnp.where(has_left & has, diag[end, 0].astype(F32), 0.0)
        dr = jnp.where(has_right & has, diag[end, 1].astype(F32), 0.0)
        plane_l = pltpu.roll(jnp.where(lane[0:1] < LANES // 2, own, dl), (j * SLOT + LEFT) % LANES, 1)
        plane_r = pltpu.roll(jnp.where(lane[0:1] < LANES // 2, dr, own), (j * SLOT + RIGHT) % LANES, 1)
        here = slot16 == j
        lf[tile] = jnp.where(here, plane_l, pltpu.roll(lf[other], shift, 1))
        rf[tile] = jnp.where(here, plane_r, pltpu.roll(rf[other], shift, 1))

    def choose(i, _):
        sv = jnp.zeros((8, LANES), I32)
        for j in range(SLOTS):
            sv = jnp.where(slot == j, skew[0, base + GROUP * j + i], sv)
        use_right = ((sv >= 1) | ((sv >= -1) & (kk < SLOT // 2)))[0:1]
        center = jnp.where(use_right, rf[i + 1], lf[i + 1])
        dh[i, PAD : PAD + rows, :] = center
        sd[i] = center.astype(BF)
        zph[i] = jnp.where(use_right, rf[i + 2], lf[i + 2])
        zmh[i] = jnp.where(use_right, rf[i], lf[i])
        tl = jnp.where(kk16 < LEFT, rt12[i].astype(F32), pt12[i].astype(F32))
        tr = jnp.where(kk16 < RIGHT, pt4[i].astype(F32), rt4[i].astype(F32))
        th[i] = jnp.where(use_right, tr, tl)
        return 0

    lax.fori_loop(0, GROUP, choose, 0)

    def halo_step(i, _):
        gx_ref[...] = jnp.dot(sd[i], grad[...], preferred_element_type=F32)
        for r in range(0, rows, 16):
            q = PAD + r
            values = classify(
                dh[i, q : q + 16, :], dh[i, q - 1 : q + 15, :], dh[i, q + 1 : q + 17, :],
                zmh[i, r : r + 16, :], zph[i, r : r + 16, :],
                gx_ref[r : r + 16, :], th[i, r : r + 16, :], words,
            )
            for c in range(4):
                vh[i, c, r : r + 16, :] = values[c].astype(BF)
        return 0

    lax.fori_loop(0, GROUP, halo_step, 0)

    back = skew[0, 0] > 0
    floor_u = jnp.where(back, 0.0, 1.0)
    def shear(g, place):
        for i in range(GROUP):
            z = g * GROUP + i
            lhs = jnp.concatenate(
                [vx[z].reshape(4 * rows, LANES), vh[i].reshape(4 * rows, LANES)], 1
            )
            y = round_bf(jnp.dot(lhs, wall[z], preferred_element_type=F32))
            for c in range(4):
                sheared[place, i, c, PAD : PAD + rows, :] = y[c * rows : (c + 1) * rows]

    carry[0:3] = jnp.zeros((3, rows, LANES), F32)
    carry[3] = jnp.ones((rows, LANES), F32)

    def composite(g, place):
        taps = []
        for i in range(GROUP):
            z = g * GROUP + i
            taps.append((skew[1, base + z], weights(1, z)))
        for r in range(0, rows, 8):
            acc = [carry[c, r : r + 8, :] for c in range(4)]
            for i in range(GROUP):
                t, (b0, b1) = taps[i]
                sample = [
                    b0 * sheared[place, i, c, pl.ds(PAD + r + t, 8), :]
                    + b1 * sheared[place, i, c, pl.ds(PAD + r + t + 1, 8), :]
                    for c in range(4)
                ]
                keep = 1.0 - sample[3]
                u = jnp.maximum(keep, floor_u)
                v = jnp.where(back, 1.0, acc[3])
                for c in range(3):
                    acc[c] = acc[c] * u + v * sample[c]
                acc[3] = acc[3] * keep
            for c in range(4):
                carry[c, r : r + 8, :] = acc[c]

    groups = depth // GROUP
    shear(0, 0)

    def fused(g, _):
        shear(g, lax.rem(g, 2))
        composite(g - 1, lax.rem(g + 1, 2))
        return 0

    lax.fori_loop(1, groups, fused, 0)
    composite(groups - 1, (groups - 1) % 2)

    top = iota((8, LANES), 0) < 4

    def halves(k, _):
        at = pl.ds(pl.multiple_of(k * 8, 8), 8)
        v = [carry[c, at, :] for c in range(4)]
        for p in range(2):
            hbuf[0, k, p] = jnp.where(top, v[2 * p], pltpu.roll(v[2 * p + 1], 4, 0))
            hbuf[1, k, p] = jnp.where(top, pltpu.roll(v[2 * p], 4, 0), v[2 * p + 1])
        return 0

    lax.fori_loop(0, chips, halves, 0)
    swap = pltpu.make_async_remote_copy(
        src_ref=hbuf.at[1 - core], dst_ref=hrecv, send_sem=pair_send, recv_sem=pair_recv,
        device_id=(col, pair), device_id_type=MESH,
    )
    swap.start()
    swap.wait_recv()
    mine_near = (core == 0) != back

    def join(k, _):
        mine = [hbuf[core, k, p] for p in range(2)]
        other = [hrecv[k, p] for p in range(2)]
        near = [jnp.where(mine_near, mine[p], other[p]) for p in range(2)]
        far = [jnp.where(mine_near, other[p], mine[p]) for p in range(2)]
        through = jnp.where(top, pltpu.roll(near[1], 4, 0), near[1])
        comb[k, 0] = near[0] + through * far[0]
        comb[k, 1] = jnp.where(top, near[1] + through * far[1], through * far[1])
        return 0

    lax.fori_loop(0, chips, join, 0)

    def out_copy(o):
        to = lax.rem(chip + o, chips)
        return pltpu.make_async_remote_copy(
            src_ref=comb.at[to], dst_ref=frecv.at[chip],
            send_sem=out_send.at[o], recv_sem=out_recv.at[o],
            device_id=(col, to * 2 + core), device_id_type=MESH,
        )

    lax.fori_loop(1, chips, lambda o, _: (out_copy(o).start(), 0)[1], 0)
    frecv[chip] = comb[chip]

    def arrive(o, _):
        pltpu.make_async_remote_copy(
            src_ref=comb.at[chip], dst_ref=frecv.at[lax.rem(chip + chips - o, chips)],
            send_sem=out_send.at[o], recv_sem=out_recv.at[o],
            device_id=(col, dep), device_id_type=MESH,
        ).wait_recv()
        return 0

    lax.fori_loop(1, chips, arrive, 0)

    def final(n, state):
        s0, s1, through = state
        k = jnp.where(back, chips - 1 - n, n)
        v0, v1 = frecv[k, 0], frecv[k, 1]
        s0 = s0 + through * v0
        s1 = s1 + through * jnp.where(top, v1, 1.0 - v1)
        through = through * jnp.where(top, pltpu.roll(v1, 4, 0), v1)
        return s0, s1, through

    zero = jnp.zeros((8, LANES), F32)
    s0, s1, _ = lax.fori_loop(0, chips, final, (zero, zero, zero + 1.0))
    out[0] = s0[0:4]
    out[1] = s0[4:8]
    out[2] = s1[0:4]
    out[3] = s1[4:8]

    for copy in planes + packs + [swap]:
        copy.wait_send()
    lax.fori_loop(1, chips, lambda o, _: (out_copy(o).wait_send(), 0)[1], 0)


def on_device(density, temperature, absorption, glow, skew, frac):
    depth, rows, _ = density.shape
    ndep = lax.axis_size("depth")
    chips = ndep // 2
    vmem = lambda *shape, dtype=F32: pltpu.VMEM(shape, dtype)
    tile = (rows, LANES)
    dma = pltpu.SemaphoreType.DMA
    scratch = [
        vmem(depth + 2, *tile, dtype=BF), vmem(depth, *tile, dtype=BF),
        vmem(depth + 2, rows + 16, LANES), vmem(2, 2, *tile, dtype=BF),
    ]
    scratch += [vmem(GROUP, *tile, dtype=BF)] * 8
    scratch += [
        vmem(GROUP + 2, *tile), vmem(GROUP + 2, *tile), vmem(GROUP, *tile, dtype=BF),
        vmem(GROUP, rows + 16, LANES), vmem(GROUP, *tile), vmem(GROUP, *tile), vmem(GROUP, *tile),
        vmem(*tile), vmem(depth, 4, *tile, dtype=BF), vmem(GROUP, 4, *tile, dtype=BF),
        vmem(SLOTS * LANES, 2 * LANES, dtype=BF), vmem(LANES, LANES, dtype=BF),
        vmem(depth, 2 * LANES, LANES, dtype=BF),
        vmem(2, GROUP, 4, rows + 24, LANES), vmem(4, *tile),
        vmem(2, chips, 2, 8, LANES), vmem(chips, 2, 8, LANES),
        vmem(chips, 2, 8, LANES), vmem(chips, 2, 8, LANES),
        dma((2,)), dma((2, 3)), dma((2, 3)), dma((4,)), dma((4,)), dma, dma,
        dma((chips,)), dma((chips,)),
    ]
    smem = pl.BlockSpec(memory_space=pltpu.SMEM)
    inside = pl.BlockSpec(memory_space=pltpu.VMEM)
    anywhere = pl.BlockSpec(memory_space=pl.ANY)
    return pl.pallas_call(
        kernel,
        out_shape=jax.ShapeDtypeStruct((4, rows // ndep, LANES), F32),
        in_specs=[smem, smem, inside, anywhere, anywhere],
        out_specs=inside,
        scratch_shapes=scratch,
        compiler_params=pltpu.CompilerParams(
            collective_id=0, has_side_effects=True, vmem_limit_bytes=48 * 2 ** 20
        ),
    )(skew, frac, table_words(absorption, glow), density, temperature)


def solution(mesh):
    in_specs = (P("depth", None, "cols"), P("depth", None, "cols"), P(), P(), P(), P())
    out_specs = P(None, "depth", "cols")
    return jax.shard_map(
        on_device, mesh=mesh, in_specs=in_specs, out_specs=out_specs, check_vma=False
    )
```

```python
import functools
import math

import jax
import jax.numpy as jnp
from jax import lax
from jax.experimental import pallas as pl
from jax.experimental.pallas import tpu as pltpu
from jax.sharding import PartitionSpec as P

MESH = pl.DeviceIdType.MESH
BF = jnp.bfloat16
F32 = jnp.float32
I32 = jnp.int32
LANES = 128
PAD = 8
GROUP = 4
SLOT = 16
SLOTS = 8
UNROLL = 4
LEFT = 12
RIGHT = 4
NINTH = 14
SH = 8

ROOT = math.sqrt(0.7) * 2.0 ** -5
KX, KY, KZ = 0.48 * ROOT, 0.6 * ROOT, 0.64 * ROOT
AMBIENT = 0.3 * 2.0 ** -10
MAGIC0 = 1.5 * 2.0 ** 33
MAGIC1 = 1.5 * 2.0 ** 35
BIAS = 10240.0 * 1024.0
EXPO = -(2.0 ** -32) * math.log2(math.e)
CODES, SHIFT = 2600.0, 27500.0


def iota(shape, dim):
    return lax.broadcasted_iota(I32, shape, dim)


def table_words(absorption, glow):
    a = absorption.astype(F32) * 2.0 ** 22
    g = glow.astype(F32) * 2.0 ** 10
    w0 = (a - 10240.0) * 1024.0 + (g[0:1] - 612.0)
    w1 = g[1:2] * 4096.0 + g[2:3]
    parts = [w0[:, :LANES], w0[:, LANES:], w1[:, :LANES], w1[:, LANES:]]
    return [jnp.broadcast_to(p, (8, LANES)) for p in parts]


def encode(x):
    code = jnp.floor(jnp.log2(x) * CODES + (SHIFT + 0.5))
    return jnp.clip(code, -32767.0, 32767.0).astype(I32).astype(jnp.int16)


def decode(code):
    c = code.astype(I32).astype(F32)
    return jnp.where(c > -32767.0, jnp.exp2((c - SHIFT) * (1.0 / CODES)), 0.0)


def round_bf(x):
    return x.astype(BF).astype(F32)


def classify(d, up, down, zm, zp, gx, t, words):
    gy = down - up
    gz = zp - zm
    f = KX * gx + KY * gy + KZ * gz
    length = gx * gx + gy * gy + gz * gz + 1.0
    shade = AMBIENT + f * f * pl.reciprocal(length, approx=True)
    index = jnp.minimum((t * 128.0 - 64.0).astype(I32), 255)
    high = index >= LANES
    low_bits = index & (LANES - 1)

    def pick(word):
        table = jnp.concatenate([word] * (index.shape[0] // 8), 0)
        return jnp.take_along_axis(table, low_bits, axis=1, mode="promise_in_bounds")

    w0 = jnp.where(high, pick(words[1]), pick(words[0]))
    w1 = jnp.where(high, pick(words[3]), pick(words[2]))
    a = (w0 + MAGIC0) - (MAGIC0 - BIAS)
    g0 = (w0 - a) + (612.0 + BIAS)
    g1 = (w1 + MAGIC1) - MAGIC1
    g2 = w1 - g1
    alpha = 1.0 - jnp.exp2(a * (d * EXPO))
    p = alpha * shade * t
    return p * g0, (p * 2.0 ** -12) * g1, p * g2, alpha


def kernel(
    skew_in, frac_in, absorption, glow, dens, temp, out,
    skew, frac, absorb_v, glow_v,
    dv, tv, df, corner_out, corner_in,
    pd12, pd4, rd12, rd4, own_t, pt_r, pt_l, rt_l, rt_r,
    lf, rf, sd, dh, zph, zmh, th,
    gx_ref, vx, vh, sel_d, sel_t, sel_n, grad, wall, sheared, carry,
    hbuf, hrecv, comb, frecv,
    local_sem, plane_send, plane_recv, diag_send, diag_recv, pack_send, pack_recv, pair_send, pair_recv,
    out_send, out_recv,
):
    depth, rows, _ = tv.shape
    chips = comb.shape[0]
    col, dep = lax.axis_index("cols"), lax.axis_index("depth")
    ncol, ndep = lax.axis_size("cols"), lax.axis_size("depth")
    chip, core = dep // 2, dep % 2
    left, right = lax.rem(col + ncol - 1, ncol), lax.rem(col + 1, ncol)
    lower, upper = lax.rem(dep + ndep - 1, ndep), lax.rem(dep + 1, ndep)
    pair = dep + 1 - 2 * core
    base = dep * depth

    barrier = pltpu.get_barrier_semaphore()
    for c in (left, col, right):
        for e in (lower, dep, upper):
            if c is col and e is dep:
                continue
            pl.semaphore_signal(barrier, inc=1, device_id=(c, e), device_id_type=MESH)

    def greet(o, _):
        other = lax.rem(chip + o, chips) * 2 + core
        pl.semaphore_signal(barrier, inc=1, device_id=(col, other), device_id_type=MESH)
        return 0

    lax.fori_loop(1, chips, greet, 0)

    small = [
        pltpu.make_async_copy(a, b, local_sem.at[2 + n])
        for n, (a, b) in enumerate(
            ((skew_in, skew), (frac_in, frac), (absorption, absorb_v), (glow, glow_v))
        )
    ]
    for copy in small:
        copy.start()
    dens_in = pltpu.make_async_copy(dens, dv.at[pl.ds(1, depth)], local_sem.at[0])
    temp_in = pltpu.make_async_copy(temp, tv, local_sem.at[1])
    dens_in.start()
    temp_in.start()

    lane = iota((8, LANES), 1)
    kk, slot = lane % SLOT, lane // SLOT
    gk, gc = iota((LANES, LANES), 0), iota((LANES, LANES), 1)
    grad[...] = (jnp.where(gk == gc + 1, 1.0, 0.0) - jnp.where(gk == gc - 1, 1.0, 0.0)).astype(BF)
    far = 1 << 20
    for side, move in enumerate((LEFT, RIGHT)):
        at = slice(side * LANES, (side + 1) * LANES)
        off = (gk + move) % LANES
        keep = off < SLOT
        if side:
            keep = keep & (off != NINTH)
        to_d = jnp.where(keep, off - gc, far)
        if side == 0:
            to_t = jnp.where(gk == 0, LEFT - gc, jnp.where(gk == LANES - 1, RIGHT - 1 - gc, far))
            to_n = jnp.where(gk >= LANES - SH, gk - (LANES - SH) - gc, far)
        else:
            to_t = jnp.where(gk == SH, NINTH - gc, far)
            to_n = jnp.where(gk < SH, gk - gc, far)

        def build_sel(j, _):
            def put(ref, at_row, gap, lanes):
                row = pl.ds(pl.multiple_of(at_row * LANES, LANES), LANES)
                ref[row, at] = jnp.where(gap == -lanes, 1.0, 0.0).astype(BF)

            put(sel_d, j, to_d, j * SLOT)
            put(sel_t, j, to_t, j * SLOT)
            put(sel_n, 2 * j, to_n, j * SLOT)
            put(sel_n, 2 * j + 1, to_n, j * SLOT + SH)
            return 0

        lax.fori_loop(0, SLOTS, build_sel, 0)

    def zero_df(z, _):
        df[z, 0:PAD, :] = jnp.zeros((PAD, LANES), F32)
        df[z, PAD + rows : PAD + rows + 8, :] = jnp.zeros((8, LANES), F32)
        return 0

    lax.fori_loop(0, depth + 2, zero_df, 0)

    def zero_sheared(k, _):
        for s in range(2):
            for c in range(4):
                sheared[s, k, c, 0:PAD, :] = jnp.zeros((PAD, LANES), F32)
                sheared[s, k, c, PAD + rows : PAD + rows + 16, :] = jnp.zeros((16, LANES), F32)
        dh[k, 0:PAD, :] = jnp.zeros((PAD, LANES), F32)
        dh[k, PAD + rows : PAD + rows + 8, :] = jnp.zeros((8, LANES), F32)
        return 0

    lax.fori_loop(0, GROUP, zero_sheared, 0)

    for copy in small:
        copy.wait()
    def weights(row, z):
        part = jnp.full((8, LANES), frac[row, base + z], F32)
        return (1.0 - part).astype(BF).astype(F32), part.astype(BF).astype(F32)

    gap = jnp.where((gk > 0) & (gk < LANES - 1), gk - gc, 1000)
    hk, hc = iota((SLOT, LANES), 0), iota((SLOT, LANES), 1)

    def build_weights(z, _):
        s = skew[0, base + z]
        a0, a1 = weights(0, z)
        a0, a1 = a0[0:1], a1[0:1]
        wall[z, 0:LANES, :] = jnp.where(gap == s, a0, jnp.where(gap == s + 1, a1, 0.0)).astype(BF)
        wall[z, LANES:, :] = jnp.zeros((LANES, LANES), BF)
        use_right = (s >= 1) | ((s >= -1) & (hk < SLOT // 2))
        hcol = jnp.where(use_right, hk + (LANES - RIGHT), hk - LEFT)
        valid = (hcol <= 0) | (hcol >= LANES - 1)
        hgap = jnp.where(valid, hcol - hc, 1000)
        at = pl.ds(pl.multiple_of(LANES + (z // GROUP) * SLOT, SLOT), SLOT)
        wall[z, at, :] = jnp.where(hgap == s, a0, jnp.where(hgap == s + 1, a1, 0.0)).astype(BF)
        return 0

    lax.fori_loop(0, depth, build_weights, 0)

    words = table_words(absorb_v[...], glow_v[...])
    def widen(z, _):
        df[z, PAD : PAD + rows, :] = dv[z].astype(F32)
        return 0

    def pack():
        def wide(ref, first):
            parts = [ref[pl.ds(first + GROUP * j, GROUP)] for j in range(SLOTS)]
            return jnp.concatenate([p.reshape(GROUP * rows, LANES) for p in parts], 1)

        both = jnp.dot(wide(dv, 1), sel_d[...], preferred_element_type=F32)
        more = jnp.dot(wide(tv, 0), sel_t[...], preferred_element_type=F32)
        for i in range(GROUP):
            at = slice(i * rows, (i + 1) * rows)
            pd12[i] = both[at, :LANES].astype(BF)
            pd4[i] = (both[at, LANES:] + more[at, LANES:]).astype(BF)
            own_t[i] = more[at, :LANES]

    def pack_narrow():
        parts = [
            jnp.concatenate([tv[GROUP * j + 2 * h + half] for h in range(2)], 0)
            for j in range(SLOTS) for half in range(2)
        ]
        both = jnp.dot(jnp.concatenate(parts, 1), sel_n[...], preferred_element_type=F32).astype(BF)
        for h in range(2):
            pt_r[h] = both[h * rows : (h + 1) * rows, :LANES]
            pt_l[h] = both[h * rows : (h + 1) * rows, LANES:]

    def fold(end, m, tile, source):
        folded = jnp.zeros((SLOT, LANES), F32)
        for k in range(rows // SLOT):
            part = tile[k * SLOT : (k + 1) * SLOT, :].astype(F32)
            folded = jnp.where(slot[0:1] == k, pltpu.roll(part, (k - source) % SLOTS * SLOT, 1), folded)
        corner_out[end, m] = folded.astype(BF)

    def unfold(end, m, target):
        part = corner_in[end, m].astype(F32)
        parts = [pltpu.roll(part, (target - k) % SLOTS * SLOT, 1) for k in range(rows // SLOT)]
        return jnp.concatenate(parts, 0)

    def send_pack(n, p, r, c):
        copy = pltpu.make_async_remote_copy(
            src_ref=p, dst_ref=r, send_sem=pack_send.at[n], recv_sem=pack_recv.at[n],
            device_id=(c, dep), device_id_type=MESH,
        )
        copy.start()
        return copy

    def main_step(n, also=None):
        places = [lax.rem(n * UNROLL + u + 1, depth) for u in range(UNROLL)]
        for u, z in enumerate(places):
            gx_ref[u] = jnp.dot(dv[z + 1], grad[...], preferred_element_type=F32)
        if also is not None:
            also()
        for u, z in enumerate(places):
            for r in range(0, rows, 16):
                q = PAD + r
                values = classify(
                    df[z + 1, q : q + 16, :], df[z + 1, q - 1 : q + 15, :],
                    df[z + 1, q + 1 : q + 17, :],
                    df[z, q : q + 16, :], df[z + 2, q : q + 16, :],
                    gx_ref[u, r : r + 16, :], tv[z, r : r + 16, :].astype(F32), words,
                )
                for c in range(4):
                    vx[z, c, r : r + 16, :] = values[c].astype(BF)

    dens_in.wait()
    lax.fori_loop(1, depth + 1, widen, 0)
    temp_in.wait()
    main_step(0, pack)

    pl.semaphore_wait(barrier, 8 + chips - 1)

    packs = [send_pack(0, pd12, rd12, right), send_pack(1, pd4, rd4, left)]
    planes, corners = [], []
    for n, (e, plane, end) in enumerate(((upper, depth - 1, 0), (lower, 0, 1))):
        planes.append(
            pltpu.make_async_remote_copy(
                src_ref=dens.at[plane], dst_ref=dv.at[end * (depth + 1)],
                send_sem=plane_send.at[n], recv_sem=plane_recv.at[n],
                device_id=(col, e), device_id_type=MESH,
            )
        )
        planes[-1].start()
        for m, (tiles, c) in enumerate(((pd12, right), (pd4, left))):
            fold(end, m, tiles.at[(GROUP - 1) * (1 - end)], (SLOTS - 1) * (1 - end))
            corners.append(
                pltpu.make_async_remote_copy(
                    src_ref=corner_out.at[end, m], dst_ref=corner_in.at[end, m],
                    send_sem=diag_send.at[n, m], recv_sem=diag_recv.at[n, m],
                    device_id=(c, e), device_id_type=MESH,
                )
            )
            corners[-1].start()
    main_step(1, pack_narrow)
    packs += [send_pack(2, pt_r, rt_l, right), send_pack(3, pt_l, rt_r, left)]
    blocks = depth // UNROLL
    lax.fori_loop(2, blocks - 1, lambda n, _: (main_step(n), 0)[1], 0)
    for copy in planes:
        copy.wait_recv()
    df[0, PAD : PAD + rows, :] = jnp.where(dep > 0, dv[0].astype(F32), 0.0)
    df[depth + 1, PAD : PAD + rows, :] = jnp.where(dep < ndep - 1, dv[depth + 1].astype(F32), 0.0)
    main_step(blocks - 1)

    for copy in packs + corners:
        copy.wait_recv()
    kk16, slot16 = kk[0:1], slot[0:1]
    has_left, has_right = col > 0, col < ncol - 1

    def windows(i, _):
        l = jnp.where(kk16 < LEFT, jnp.where(has_left, rd12[i].astype(F32), 0.0), pd12[i].astype(F32))
        r = jnp.where(kk16 < RIGHT, pd4[i].astype(F32), jnp.where(has_right, rd4[i].astype(F32), 0.0))
        lf[i + 1] = l
        rf[i + 1] = r
        return 0

    lax.fori_loop(0, GROUP, windows, 0)
    for end, j, tile, other, shift, has in (
        (0, 0, 0, GROUP, SLOT, dep > 0),
        (1, SLOTS - 1, GROUP + 1, 1, LANES - SLOT, dep < ndep - 1),
    ):
        own = df[end * (depth + 1), PAD : PAD + rows, :]
        here = slot16 == j
        for m, (move, window, has_side) in enumerate(((LEFT, lf, has_left), (RIGHT, rf, has_right))):
            side = jnp.where(has_side & has, unfold(end, m, j), 0.0)
            mine = here & ((kk16 >= LEFT) if m == 0 else (kk16 < RIGHT))
            moved = jnp.where(here, side, pltpu.roll(window[other], shift, 1))
            window[tile] = jnp.where(mine, pltpu.roll(own, (j * SLOT + move) % LANES, 1), moved)

    def choose(i, _):
        sv = jnp.zeros((8, LANES), I32)
        for j in range(SLOTS):
            sv = jnp.where(slot == j, skew[0, base + GROUP * j + i], sv)
        use_right = ((sv >= 1) | ((sv >= -1) & (kk < SLOT // 2)))[0:1]
        center = jnp.where(use_right, rf[i + 1], lf[i + 1])
        dh[i, PAD : PAD + rows, :] = center
        sd[i] = center.astype(BF)
        zph[i] = jnp.where(use_right, rf[i + 2], lf[i + 2])
        zmh[i] = jnp.where(use_right, rf[i], lf[i])
        turn = jnp.where(lax.rem(i, 2) == 0, RIGHT, LANES - RIGHT)
        tl = pltpu.roll(rt_l[i // 2].astype(F32), turn, 1)
        tr = pltpu.roll(rt_r[i // 2].astype(F32), turn, 1)
        ninth = pltpu.roll(rd4[i].astype(F32), LANES - NINTH + LEFT, 1)
        tl = jnp.where(kk16 == LEFT, own_t[i], tl)
        tr = jnp.where(kk16 == RIGHT - 1, own_t[i], jnp.where(kk16 == LEFT, ninth, tr))
        th[i] = jnp.where(use_right, tr, tl)
        return 0

    lax.fori_loop(0, GROUP, choose, 0)

    def halo_step(i, _):
        gx_ref[0] = jnp.dot(sd[i], grad[...], preferred_element_type=F32)
        for r in range(0, rows, 16):
            q = PAD + r
            values = classify(
                dh[i, q : q + 16, :], dh[i, q - 1 : q + 15, :], dh[i, q + 1 : q + 17, :],
                zmh[i, r : r + 16, :], zph[i, r : r + 16, :],
                gx_ref[0, r : r + 16, :], th[i, r : r + 16, :], words,
            )
            for c in range(4):
                vh[i, c, r : r + 16, :] = values[c].astype(BF)
        return 0

    lax.fori_loop(0, GROUP, halo_step, 0)

    back = skew[0, 0] > 0
    floor_u = jnp.where(back, 0.0, 1.0)
    def shear(g, place, quarters=range(GROUP)):
        for i in quarters:
            z = g * GROUP + i
            lhs = jnp.concatenate(
                [vx[z].reshape(4 * rows, LANES), vh[i].reshape(4 * rows, LANES)], 1
            )
            y = round_bf(jnp.dot(lhs, wall[z], preferred_element_type=F32))
            for c in range(4):
                sheared[place, i, c, PAD : PAD + rows, :] = y[c * rows : (c + 1) * rows]

    carry[0:3] = jnp.zeros((3, rows, LANES), F32)
    carry[3] = jnp.ones((rows, LANES), F32)

    def composite(g, place, quarters=range(GROUP)):
        taps = []
        for i in range(GROUP):
            z = g * GROUP + i
            taps.append((skew[1, base + z], weights(1, z)))
        tiles = rows // (8 * GROUP) if rows >= 8 * GROUP else rows // 8
        for r in [8 * (q * tiles + k) for q in quarters for k in range(tiles) if 8 * (q * tiles + k) < rows]:
            acc = [carry[c, r : r + 8, :] for c in range(4)]
            for i in range(GROUP):
                t, (b0, b1) = taps[i]
                sample = [
                    b0 * sheared[place, i, c, pl.ds(PAD + r + t, 8), :]
                    + b1 * sheared[place, i, c, pl.ds(PAD + r + t + 1, 8), :]
                    for c in range(4)
                ]
                keep = 1.0 - sample[3]
                u = jnp.maximum(keep, floor_u)
                v = jnp.where(back, 1.0, acc[3])
                for c in range(3):
                    acc[c] = acc[c] * u + v * sample[c]
                acc[3] = acc[3] * keep
            for c in range(4):
                carry[c, r : r + 8, :] = acc[c]

    groups = depth // GROUP
    shear(0, 0)

    def fused(g, _):
        for q in range(GROUP):
            shear(g, lax.rem(g, 2), (q,))
            composite(g - 1, lax.rem(g + 1, 2), (q,))
        return 0

    lax.fori_loop(1, groups, fused, 0)
    composite(groups - 1, (groups - 1) % 2)

    top = iota((8, LANES), 0) < 4

    def halves(k, _):
        at = pl.ds(pl.multiple_of(k * 8, 8), 8)
        v = [carry[c, at, :] for c in range(4)]
        for p in range(2):
            hbuf[0, k, p] = jnp.where(top, v[2 * p], pltpu.roll(v[2 * p + 1], 4, 0))
            hbuf[1, k, p] = jnp.where(top, pltpu.roll(v[2 * p], 4, 0), v[2 * p + 1])
        return 0

    lax.fori_loop(0, chips, halves, 0)
    swap = pltpu.make_async_remote_copy(
        src_ref=hbuf.at[1 - core], dst_ref=hrecv, send_sem=pair_send, recv_sem=pair_recv,
        device_id=(col, pair), device_id_type=MESH,
    )
    swap.start()
    swap.wait_recv()
    mine_near = (core == 0) != back

    def join(k, _):
        mine = [hbuf[core, k, p] for p in range(2)]
        other = [hrecv[k, p] for p in range(2)]
        near = [jnp.where(mine_near, mine[p], other[p]) for p in range(2)]
        far = [jnp.where(mine_near, other[p], mine[p]) for p in range(2)]
        through = jnp.where(top, pltpu.roll(near[1], 4, 0), near[1])
        first = near[0] + through * far[0]
        second = jnp.where(top, near[1] + through * far[1], 1.0 - through * far[1])
        comb[k] = encode(jnp.concatenate([first, second], 0))
        return 0

    lax.fori_loop(0, chips, join, 0)

    def out_copy(o):
        to = lax.rem(chip + o, chips)
        return pltpu.make_async_remote_copy(
            src_ref=comb.at[to], dst_ref=frecv.at[chip],
            send_sem=out_send.at[o], recv_sem=out_recv.at[o],
            device_id=(col, to * 2 + core), device_id_type=MESH,
        )

    lax.fori_loop(1, chips, lambda o, _: (out_copy(o).start(), 0)[1], 0)
    frecv[chip] = comb[chip]

    def arrive(o, _):
        pltpu.make_async_remote_copy(
            src_ref=comb.at[chip], dst_ref=frecv.at[lax.rem(chip + chips - o, chips)],
            send_sem=out_send.at[o], recv_sem=out_recv.at[o],
            device_id=(col, dep), device_id_type=MESH,
        ).wait_recv()
        return 0

    lax.fori_loop(1, chips, arrive, 0)

    def final(n, state):
        s0, s1, through = state
        k = jnp.where(back, chips - 1 - n, n)
        v = decode(frecv[k])
        v0, v1 = v[:8], v[8:]
        s0 = s0 + through * v0
        s1 = s1 + through * v1
        through = through * (1.0 - jnp.where(top, pltpu.roll(v1, 4, 0), v1))
        return s0, s1, through

    zero = jnp.zeros((8, LANES), F32)
    s0, s1, _ = lax.fori_loop(0, chips, final, (zero, zero, zero + 1.0))
    out[0] = s0[0:4]
    out[1] = s0[4:8]
    out[2] = s1[0:4]
    out[3] = s1[4:8]

    for copy in planes + corners + packs + [swap]:
        copy.wait_send()
    lax.fori_loop(1, chips, lambda o, _: (out_copy(o).wait_send(), 0)[1], 0)


def on_device(density, temperature, absorption, glow, skew, frac):
    depth, rows, _ = density.shape
    ndep = lax.axis_size("depth")
    chips = ndep // 2
    vmem = lambda *shape, dtype=F32: pltpu.VMEM(shape, dtype)
    tile = (rows, LANES)
    dma = pltpu.SemaphoreType.DMA
    scratch = [
        pltpu.SMEM(skew.shape, I32), pltpu.SMEM(frac.shape, F32),
        vmem(1, 2 * LANES, dtype=BF), vmem(3, 2 * LANES, dtype=BF),
        vmem(depth + 2, *tile, dtype=BF), vmem(depth, *tile, dtype=BF),
        vmem(depth + 2, rows + 16, LANES), vmem(2, 2, SLOT, LANES, dtype=BF), vmem(2, 2, SLOT, LANES, dtype=BF),
    ]
    scratch += [vmem(GROUP, *tile, dtype=BF)] * 4 + [vmem(GROUP, *tile)]
    scratch += [vmem(GROUP // 2, *tile, dtype=BF)] * 4
    scratch += [
        vmem(GROUP + 2, *tile), vmem(GROUP + 2, *tile), vmem(GROUP, *tile, dtype=BF),
        vmem(GROUP, rows + 16, LANES), vmem(GROUP, *tile), vmem(GROUP, *tile), vmem(GROUP, *tile),
        vmem(UNROLL, *tile), vmem(depth, 4, *tile, dtype=BF), vmem(GROUP, 4, *tile, dtype=BF),
        vmem(SLOTS * LANES, 2 * LANES, dtype=BF), vmem(SLOTS * LANES, 2 * LANES, dtype=BF),
        vmem(SLOTS * 2 * LANES, 2 * LANES, dtype=BF), vmem(LANES, LANES, dtype=BF),
        vmem(depth, 2 * LANES, LANES, dtype=BF),
        vmem(2, GROUP, 4, rows + 24, LANES), vmem(4, *tile),
        vmem(2, chips, 2, 8, LANES), vmem(chips, 2, 8, LANES),
        vmem(chips, 16, LANES, dtype=jnp.int16), vmem(chips, 16, LANES, dtype=jnp.int16),
        dma((6,)), dma((2,)), dma((2,)), dma((2, 2)), dma((2, 2)), dma((4,)), dma((4,)), dma, dma,
        dma((chips,)), dma((chips,)),
    ]
    inside = pl.BlockSpec(memory_space=pltpu.VMEM)
    anywhere = pl.BlockSpec(memory_space=pltpu.HBM)
    return pl.pallas_call(
        kernel,
        out_shape=jax.ShapeDtypeStruct((4, rows // ndep, LANES), F32),
        in_specs=[anywhere] * 6,
        out_specs=inside,
        scratch_shapes=scratch,
        compiler_params=pltpu.CompilerParams(
            collective_id=0, has_side_effects=True, vmem_limit_bytes=64 * 2 ** 20
        ),
    )(skew, frac, absorption[None], glow, density, temperature)


def solution(mesh):
    in_specs = (P("depth", None, "cols"), P("depth", None, "cols"), P(), P(), P(), P())
    out_specs = P(None, "depth", "cols")
    return jax.shard_map(
        on_device, mesh=mesh, in_specs=in_specs, out_specs=out_specs, check_vma=False
    )
```

```python
import functools
import math

import jax
import jax.numpy as jnp
from jax import lax
from jax.experimental import pallas as pl
from jax.experimental.pallas import tpu as pltpu
from jax.sharding import PartitionSpec as P

MESH = pl.DeviceIdType.MESH
BF = jnp.bfloat16
F32 = jnp.float32
I32 = jnp.int32
LANES = 128
PAD = 8
GROUP = 4
SLOT = 16
SLOTS = 8
UNROLL = 4
LEFT = 12
RIGHT = 4
NINTH = 14
SH = 8

ROOT = math.sqrt(0.7) * 2.0 ** -5
KX, KY, KZ = 0.48 * ROOT, 0.6 * ROOT, 0.64 * ROOT
AMBIENT = 0.3 * 2.0 ** -10
MAGIC0 = 1.5 * 2.0 ** 33
MAGIC1 = 1.5 * 2.0 ** 35
BIAS = 10240.0 * 1024.0
EXPO = -(2.0 ** -32) * math.log2(math.e)
CODES, SHIFT = 2600.0, 27500.0


def iota(shape, dim):
    return lax.broadcasted_iota(I32, shape, dim)


def table_words(absorption, glow):
    a = absorption.astype(F32) * 2.0 ** 22
    g = glow.astype(F32) * 2.0 ** 10
    w0 = (a - 10240.0) * 1024.0 + (g[0:1] - 612.0)
    w1 = g[1:2] * 4096.0 + g[2:3]
    parts = [w0[:, :LANES], w0[:, LANES:], w1[:, :LANES], w1[:, LANES:]]
    return [jnp.broadcast_to(p, (8, LANES)) for p in parts]


def encode(x):
    code = jnp.floor(jnp.log2(x) * CODES + (SHIFT + 0.5))
    return jnp.clip(code, -32767.0, 32767.0).astype(I32).astype(jnp.int16)


def decode(code):
    c = code.astype(I32).astype(F32)
    return jnp.where(c > -32767.0, jnp.exp2((c - SHIFT) * (1.0 / CODES)), 0.0)


def repeat(low, high, body, unroll):
    while (high - low) % unroll:
        unroll -= 1

    def step(n, _):
        for u in range(unroll):
            body(low + n * unroll + u, 0)
        return 0

    if unroll == high - low:
        step(0, 0)
    else:
        lax.fori_loop(0, (high - low) // unroll, step, 0)


def round_bf(x):
    return x.astype(BF).astype(F32)


def classify(d, up, down, zm, zp, gx, t, words):
    gy = down - up
    gz = zp - zm
    f = KX * gx + KY * gy + KZ * gz
    length = gx * gx + gy * gy + gz * gz + 1.0
    shade = AMBIENT + f * f * pl.reciprocal(length, approx=True)
    index = jnp.minimum((t * 128.0 - 64.0).astype(I32), 255)
    high = index >= LANES
    low_bits = index & (LANES - 1)

    def pick(word):
        table = jnp.concatenate([word] * (index.shape[0] // 8), 0)
        return jnp.take_along_axis(table, low_bits, axis=1, mode="promise_in_bounds")

    w0 = jnp.where(high, pick(words[1]), pick(words[0]))
    w1 = jnp.where(high, pick(words[3]), pick(words[2]))
    a = (w0 + MAGIC0) - (MAGIC0 - BIAS)
    g0 = (w0 - a) + (612.0 + BIAS)
    g1 = (w1 + MAGIC1) - MAGIC1
    g2 = w1 - g1
    alpha = 1.0 - jnp.exp2(a * (d * EXPO))
    p = alpha * shade * t
    return p * g0, (p * 2.0 ** -12) * g1, p * g2, alpha


def kernel(
    skew_in, frac_in, absorption, glow, dens, temp, out,
    skew, frac, absorb_v, glow_v,
    dv, tv, df, corner_out, corner_in,
    pd12, pd4, rd12, rd4, own_t, pt_r, pt_l, rt_l, rt_r,
    lf, rf, sd, dh, zph, zmh, th,
    gx_ref, vx, vh, sel_d, sel_t, sel_n, grad, wall, sheared, carry,
    hbuf, hrecv, comb, frecv,
    local_sem, plane_send, plane_recv, diag_send, diag_recv, pack_send, pack_recv, pair_send, pair_recv,
    out_send, out_recv,
):
    depth, rows, _ = tv.shape
    chips = comb.shape[0]
    col, dep = lax.axis_index("cols"), lax.axis_index("depth")
    ncol, ndep = lax.axis_size("cols"), lax.axis_size("depth")
    chip, core = dep // 2, dep % 2
    left, right = lax.rem(col + ncol - 1, ncol), lax.rem(col + 1, ncol)
    lower, upper = lax.rem(dep + ndep - 1, ndep), lax.rem(dep + 1, ndep)
    pair = dep + 1 - 2 * core
    base = dep * depth

    barrier = pltpu.get_barrier_semaphore()
    for c in (left, col, right):
        for e in (lower, dep, upper):
            if c is col and e is dep:
                continue
            pl.semaphore_signal(barrier, inc=1, device_id=(c, e), device_id_type=MESH)

    def greet(o, _):
        other = lax.rem(chip + o, chips) * 2 + core
        pl.semaphore_signal(barrier, inc=1, device_id=(col, other), device_id_type=MESH)
        return 0

    lax.fori_loop(1, chips, greet, 0)

    small = [
        pltpu.make_async_copy(a, b, local_sem.at[2 + n])
        for n, (a, b) in enumerate(
            ((skew_in, skew), (frac_in, frac), (absorption, absorb_v), (glow, glow_v))
        )
    ]
    for copy in small:
        copy.start()
    dens_in = pltpu.make_async_copy(dens, dv.at[pl.ds(1, depth)], local_sem.at[0])
    temp_in = pltpu.make_async_copy(temp, tv, local_sem.at[1])
    dens_in.start()
    temp_in.start()

    lane = iota((8, LANES), 1)
    kk, slot = lane % SLOT, lane // SLOT
    gk, gc = iota((LANES, LANES), 0), iota((LANES, LANES), 1)
    grad[...] = (jnp.where(gk == gc + 1, 1.0, 0.0) - jnp.where(gk == gc - 1, 1.0, 0.0)).astype(BF)
    far = 1 << 20
    for side, move in enumerate((LEFT, RIGHT)):
        at = slice(side * LANES, (side + 1) * LANES)
        off = (gk + move) % LANES
        keep = off < SLOT
        if side:
            keep = keep & (off != NINTH)
        to_d = jnp.where(keep, off - gc, far)
        if side == 0:
            to_t = jnp.where(gk == 0, LEFT - gc, jnp.where(gk == LANES - 1, RIGHT - 1 - gc, far))
            to_n = jnp.where(gk >= LANES - SH, gk - (LANES - SH) - gc, far)
        else:
            to_t = jnp.where(gk == SH, NINTH - gc, far)
            to_n = jnp.where(gk < SH, gk - gc, far)

        def build_sel(j, _):
            def put(ref, at_row, gap, lanes):
                row = pl.ds(pl.multiple_of(at_row * LANES, LANES), LANES)
                ref[row, at] = jnp.where(gap == -lanes, 1.0, 0.0).astype(BF)

            put(sel_d, j, to_d, j * SLOT)
            put(sel_t, j, to_t, j * SLOT)
            put(sel_n, 2 * j, to_n, j * SLOT)
            put(sel_n, 2 * j + 1, to_n, j * SLOT + SH)
            return 0

        repeat(0, SLOTS, build_sel, 2)

    def zero_df(z, _):
        df[z, 0:PAD, :] = jnp.zeros((PAD, LANES), F32)
        df[z, PAD + rows : PAD + rows + 8, :] = jnp.zeros((8, LANES), F32)
        return 0

    repeat(0, depth + 2, zero_df, 17)

    def zero_sheared(k, _):
        for s in range(2):
            for c in range(4):
                sheared[s, k, c, 0:PAD, :] = jnp.zeros((PAD, LANES), F32)
                sheared[s, k, c, PAD + rows : PAD + rows + 16, :] = jnp.zeros((16, LANES), F32)
        dh[k, 0:PAD, :] = jnp.zeros((PAD, LANES), F32)
        dh[k, PAD + rows : PAD + rows + 8, :] = jnp.zeros((8, LANES), F32)
        return 0

    lax.fori_loop(0, GROUP, zero_sheared, 0)

    for copy in small:
        copy.wait()
    def weights(row, z):
        part = jnp.full((8, LANES), frac[row, base + z], F32)
        return (1.0 - part).astype(BF).astype(F32), part.astype(BF).astype(F32)

    gap = jnp.where((gk > 0) & (gk < LANES - 1), gk - gc, 1000)
    hk, hc = iota((SLOT, LANES), 0), iota((SLOT, LANES), 1)

    def build_weights(z, _):
        s = skew[0, base + z]
        a0, a1 = weights(0, z)
        a0, a1 = a0[0:1], a1[0:1]
        wall[z, 0:LANES, :] = jnp.where(gap == s, a0, jnp.where(gap == s + 1, a1, 0.0)).astype(BF)
        wall[z, LANES:, :] = jnp.zeros((LANES, LANES), BF)
        use_right = (s >= 1) | ((s >= -1) & (hk < SLOT // 2))
        hcol = jnp.where(use_right, hk + (LANES - RIGHT), hk - LEFT)
        valid = (hcol <= 0) | (hcol >= LANES - 1)
        hgap = jnp.where(valid, hcol - hc, 1000)
        at = pl.ds(pl.multiple_of(LANES + (z // GROUP) * SLOT, SLOT), SLOT)
        wall[z, at, :] = jnp.where(hgap == s, a0, jnp.where(hgap == s + 1, a1, 0.0)).astype(BF)
        return 0

    repeat(0, depth, build_weights, 4)

    words = table_words(absorb_v[...].reshape(1, 2 * LANES), glow_v[...])
    def widen(z, _):
        df[z, PAD : PAD + rows, :] = dv[z].astype(F32)
        return 0

    def pack():
        def wide(ref, first):
            parts = [ref[pl.ds(first + GROUP * j, GROUP)] for j in range(SLOTS)]
            return jnp.concatenate([p.reshape(GROUP * rows, LANES) for p in parts], 1)

        both = jnp.dot(wide(dv, 1), sel_d[...], preferred_element_type=F32)
        more = jnp.dot(wide(tv, 0), sel_t[...], preferred_element_type=F32)
        for i in range(GROUP):
            at = slice(i * rows, (i + 1) * rows)
            pd12[i] = both[at, :LANES].astype(BF)
            pd4[i] = (both[at, LANES:] + more[at, LANES:]).astype(BF)
            own_t[i] = more[at, :LANES]

    def pack_narrow():
        parts = [
            jnp.concatenate([tv[GROUP * j + 2 * h + half] for h in range(2)], 0)
            for j in range(SLOTS) for half in range(2)
        ]
        both = jnp.dot(jnp.concatenate(parts, 1), sel_n[...], preferred_element_type=F32).astype(BF)
        for h in range(2):
            pt_r[h] = both[h * rows : (h + 1) * rows, :LANES]
            pt_l[h] = both[h * rows : (h + 1) * rows, LANES:]

    def fold(end, m, tile, source):
        folded = jnp.zeros((SLOT, LANES), F32)
        for k in range(rows // SLOT):
            part = tile[k * SLOT : (k + 1) * SLOT, :].astype(F32)
            folded = jnp.where(slot[0:1] == k, pltpu.roll(part, (k - source) % SLOTS * SLOT, 1), folded)
        corner_out[end, m] = folded.astype(BF)

    def unfold(end, m, target):
        part = corner_in[end, m].astype(F32)
        parts = [pltpu.roll(part, (target - k) % SLOTS * SLOT, 1) for k in range(rows // SLOT)]
        return jnp.concatenate(parts, 0)

    def send_pack(n, p, r, c):
        copy = pltpu.make_async_remote_copy(
            src_ref=p, dst_ref=r, send_sem=pack_send.at[n], recv_sem=pack_recv.at[n],
            device_id=(c, dep), device_id_type=MESH,
        )
        copy.start()
        return copy

    def main_step(n, also=None):
        places = [lax.rem(n * UNROLL + u + 1, depth) for u in range(UNROLL)]
        for u, z in enumerate(places):
            gx_ref[u] = jnp.dot(dv[z + 1], grad[...], preferred_element_type=F32)
        if also is not None:
            also()
        for u, z in enumerate(places):
            for r in range(0, rows, 16):
                q = PAD + r
                values = classify(
                    df[z + 1, q : q + 16, :], df[z + 1, q - 1 : q + 15, :],
                    df[z + 1, q + 1 : q + 17, :],
                    df[z, q : q + 16, :], df[z + 2, q : q + 16, :],
                    gx_ref[u, r : r + 16, :], tv[z, r : r + 16, :].astype(F32), words,
                )
                for c in range(4):
                    vx[z, c, r : r + 16, :] = values[c].astype(BF)

    dens_in.wait()
    repeat(1, depth + 1, widen, 8)
    temp_in.wait()
    main_step(0, pack)

    pl.semaphore_wait(barrier, 8 + chips - 1)

    packs = [send_pack(0, pd12, rd12, right), send_pack(1, pd4, rd4, left)]
    planes, corners = [], []
    for n, (e, plane, end) in enumerate(((upper, depth - 1, 0), (lower, 0, 1))):
        planes.append(
            pltpu.make_async_remote_copy(
                src_ref=dens.at[plane], dst_ref=dv.at[end * (depth + 1)],
                send_sem=plane_send.at[n], recv_sem=plane_recv.at[n],
                device_id=(col, e), device_id_type=MESH,
            )
        )
        planes[-1].start()
        for m, (tiles, c) in enumerate(((pd12, right), (pd4, left))):
            fold(end, m, tiles.at[(GROUP - 1) * (1 - end)], (SLOTS - 1) * (1 - end))
            corners.append(
                pltpu.make_async_remote_copy(
                    src_ref=corner_out.at[end, m], dst_ref=corner_in.at[end, m],
                    send_sem=diag_send.at[n, m], recv_sem=diag_recv.at[n, m],
                    device_id=(c, e), device_id_type=MESH,
                )
            )
            corners[-1].start()
    main_step(1, pack_narrow)
    packs += [send_pack(2, pt_r, rt_l, right), send_pack(3, pt_l, rt_r, left)]
    blocks = depth // UNROLL
    lax.fori_loop(2, blocks - 1, lambda n, _: (main_step(n), 0)[1], 0)
    for copy in planes:
        copy.wait_recv()
    df[0, PAD : PAD + rows, :] = jnp.where(dep > 0, dv[0].astype(F32), 0.0)
    df[depth + 1, PAD : PAD + rows, :] = jnp.where(dep < ndep - 1, dv[depth + 1].astype(F32), 0.0)
    main_step(blocks - 1)

    for copy in packs + corners:
        copy.wait_recv()
    kk16, slot16 = kk[0:1], slot[0:1]
    has_left, has_right = col > 0, col < ncol - 1

    def windows(i, _):
        l = jnp.where(kk16 < LEFT, jnp.where(has_left, rd12[i].astype(F32), 0.0), pd12[i].astype(F32))
        r = jnp.where(kk16 < RIGHT, pd4[i].astype(F32), jnp.where(has_right, rd4[i].astype(F32), 0.0))
        lf[i + 1] = l
        rf[i + 1] = r
        return 0

    repeat(0, GROUP, windows, GROUP)
    for end, j, tile, other, shift, has in (
        (0, 0, 0, GROUP, SLOT, dep > 0),
        (1, SLOTS - 1, GROUP + 1, 1, LANES - SLOT, dep < ndep - 1),
    ):
        own = df[end * (depth + 1), PAD : PAD + rows, :]
        here = slot16 == j
        for m, (move, window, has_side) in enumerate(((LEFT, lf, has_left), (RIGHT, rf, has_right))):
            side = jnp.where(has_side & has, unfold(end, m, j), 0.0)
            mine = here & ((kk16 >= LEFT) if m == 0 else (kk16 < RIGHT))
            moved = jnp.where(here, side, pltpu.roll(window[other], shift, 1))
            window[tile] = jnp.where(mine, pltpu.roll(own, (j * SLOT + move) % LANES, 1), moved)

    def choose(i, _):
        sv = jnp.zeros((8, LANES), I32)
        for j in range(SLOTS):
            sv = jnp.where(slot == j, skew[0, base + GROUP * j + i], sv)
        use_right = ((sv >= 1) | ((sv >= -1) & (kk < SLOT // 2)))[0:1]
        center = jnp.where(use_right, rf[i + 1], lf[i + 1])
        dh[i, PAD : PAD + rows, :] = center
        sd[i] = center.astype(BF)
        zph[i] = jnp.where(use_right, rf[i + 2], lf[i + 2])
        zmh[i] = jnp.where(use_right, rf[i], lf[i])
        turn = jnp.where(lax.rem(i, 2) == 0, RIGHT, LANES - RIGHT)
        tl = pltpu.roll(rt_l[i // 2].astype(F32), turn, 1)
        tr = pltpu.roll(rt_r[i // 2].astype(F32), turn, 1)
        ninth = pltpu.roll(rd4[i].astype(F32), LANES - NINTH + LEFT, 1)
        tl = jnp.where(kk16 == LEFT, own_t[i], tl)
        tr = jnp.where(kk16 == RIGHT - 1, own_t[i], jnp.where(kk16 == LEFT, ninth, tr))
        th[i] = jnp.where(use_right, tr, tl)
        return 0

    repeat(0, GROUP, choose, GROUP)

    def halo_step(n, _):
        for u in range(2):
            gx_ref[u] = jnp.dot(sd[2 * n + u], grad[...], preferred_element_type=F32)
        for u in range(2):
            i = 2 * n + u
            for r in range(0, rows, 16):
                q = PAD + r
                values = classify(
                    dh[i, q : q + 16, :], dh[i, q - 1 : q + 15, :], dh[i, q + 1 : q + 17, :],
                    zmh[i, r : r + 16, :], zph[i, r : r + 16, :],
                    gx_ref[u, r : r + 16, :], th[i, r : r + 16, :], words,
                )
                for c in range(4):
                    vh[i, c, r : r + 16, :] = values[c].astype(BF)
        return 0

    lax.fori_loop(0, GROUP // 2, halo_step, 0)

    back = skew[0, 0] > 0

    def eye(step):
        return jnp.where(back, depth - 1 - step, step)

    def shear(g, place, quarters=range(GROUP)):
        for i in quarters:
            z = eye(g * GROUP + i)
            lhs = jnp.concatenate(
                [vx[z].reshape(4 * rows, LANES), vh[lax.rem(z, GROUP)].reshape(4 * rows, LANES)], 1
            )
            y = round_bf(jnp.dot(lhs, wall[z], preferred_element_type=F32))
            for c in range(4):
                sheared[place, i, c, PAD : PAD + rows, :] = y[c * rows : (c + 1) * rows]

    carry[0:3] = jnp.zeros((3, rows, LANES), F32)
    carry[3] = jnp.ones((rows, LANES), F32)

    def composite(g, place, quarters=range(GROUP)):
        taps = []
        for i in range(GROUP):
            z = eye(g * GROUP + i)
            taps.append((skew[1, base + z], weights(1, z)))
        tiles = rows // (8 * GROUP) if rows >= 8 * GROUP else rows // 8
        for r in [8 * (q * tiles + k) for q in quarters for k in range(tiles) if 8 * (q * tiles + k) < rows]:
            acc = [carry[c, r : r + 8, :] for c in range(4)]
            for i in range(GROUP):
                t, (b0, b1) = taps[i]
                sample = [
                    b0 * sheared[place, i, c, pl.ds(PAD + r + t, 8), :]
                    + b1 * sheared[place, i, c, pl.ds(PAD + r + t + 1, 8), :]
                    for c in range(4)
                ]
                keep = 1.0 - sample[3]
                for c in range(3):
                    acc[c] = acc[c] + acc[3] * sample[c]
                acc[3] = acc[3] * keep
            for c in range(4):
                carry[c, r : r + 8, :] = acc[c]

    groups = depth // GROUP
    shear(0, 0)

    def fused(g, _):
        for q in range(GROUP):
            shear(g, lax.rem(g, 2), (q,))
            composite(g - 1, lax.rem(g + 1, 2), (q,))
        return 0

    lax.fori_loop(1, groups, fused, 0)
    composite(groups - 1, (groups - 1) % 2)

    top = iota((8, LANES), 0) < 4

    def halves(k, _):
        at = pl.ds(pl.multiple_of(k * 8, 8), 8)
        v = [carry[c, at, :] for c in range(4)]
        for p in range(2):
            hbuf[0, k, p] = jnp.where(top, v[2 * p], pltpu.roll(v[2 * p + 1], 4, 0))
            hbuf[1, k, p] = jnp.where(top, pltpu.roll(v[2 * p], 4, 0), v[2 * p + 1])
        return 0

    repeat(0, chips, halves, chips)
    swap = pltpu.make_async_remote_copy(
        src_ref=hbuf.at[1 - core], dst_ref=hrecv, send_sem=pair_send, recv_sem=pair_recv,
        device_id=(col, pair), device_id_type=MESH,
    )
    swap.start()
    swap.wait_recv()
    mine_near = (core == 0) != back

    def join(k, _):
        mine = [hbuf[core, k, p] for p in range(2)]
        other = [hrecv[k, p] for p in range(2)]
        near = [jnp.where(mine_near, mine[p], other[p]) for p in range(2)]
        far = [jnp.where(mine_near, other[p], mine[p]) for p in range(2)]
        through = jnp.where(top, pltpu.roll(near[1], 4, 0), near[1])
        first = near[0] + through * far[0]
        second = jnp.where(top, near[1] + through * far[1], 1.0 - through * far[1])
        comb[k] = encode(jnp.concatenate([first, second], 0))
        return 0

    repeat(0, chips, join, chips)

    def out_copy(o):
        to = lax.rem(chip + o, chips)
        return pltpu.make_async_remote_copy(
            src_ref=comb.at[to], dst_ref=frecv.at[chip],
            send_sem=out_send.at[o], recv_sem=out_recv.at[o],
            device_id=(col, to * 2 + core), device_id_type=MESH,
        )

    for n in range(chips - 1):
        out_copy(chips // 2 + (n + 1) // 2 * (1 if n % 2 == 0 else -1)).start()
    frecv[chip] = comb[chip]

    def arrive(o, _):
        pltpu.make_async_remote_copy(
            src_ref=comb.at[chip], dst_ref=frecv.at[lax.rem(chip + chips - o, chips)],
            send_sem=out_send.at[o], recv_sem=out_recv.at[o],
            device_id=(col, dep), device_id_type=MESH,
        ).wait_recv()
        return 0

    lax.fori_loop(1, chips, arrive, 0)

    def final(n, state):
        s0, s1, through = state
        k = jnp.where(back, chips - 1 - n, n)
        v = decode(frecv[k])
        v0, v1 = v[:8], v[8:]
        s0 = s0 + through * v0
        s1 = s1 + through * v1
        through = through * (1.0 - jnp.where(top, pltpu.roll(v1, 4, 0), v1))
        return s0, s1, through

    zero = jnp.zeros((8, LANES), F32)
    state = (zero, zero, zero + 1.0)
    for n in range(chips):
        state = final(n, state)
    s0, s1, _ = state
    out[0] = s0[0:4]
    out[1] = s0[4:8]
    out[2] = s1[0:4]
    out[3] = s1[4:8]

    for copy in planes + corners + packs + [swap]:
        copy.wait_send()
    lax.fori_loop(1, chips, lambda o, _: (out_copy(o).wait_send(), 0)[1], 0)


def on_device(density, temperature, absorption, glow, skew, frac):
    depth, rows, _ = density.shape
    ndep = lax.axis_size("depth")
    chips = ndep // 2
    vmem = lambda *shape, dtype=F32: pltpu.VMEM(shape, dtype)
    tile = (rows, LANES)
    dma = pltpu.SemaphoreType.DMA
    scratch = [
        pltpu.SMEM(skew.shape, I32), pltpu.SMEM(frac.shape, F32),
        vmem(2 * LANES, dtype=BF), vmem(3, 2 * LANES, dtype=BF),
        vmem(depth + 2, *tile, dtype=BF), vmem(depth, *tile, dtype=BF),
        vmem(depth + 2, rows + 16, LANES), vmem(2, 2, SLOT, LANES, dtype=BF), vmem(2, 2, SLOT, LANES, dtype=BF),
    ]
    scratch += [vmem(GROUP, *tile, dtype=BF)] * 4 + [vmem(GROUP, *tile)]
    scratch += [vmem(GROUP // 2, *tile, dtype=BF)] * 4
    scratch += [
        vmem(GROUP + 2, *tile), vmem(GROUP + 2, *tile), vmem(GROUP, *tile, dtype=BF),
        vmem(GROUP, rows + 16, LANES), vmem(GROUP, *tile), vmem(GROUP, *tile), vmem(GROUP, *tile),
        vmem(UNROLL, *tile), vmem(depth, 4, *tile, dtype=BF), vmem(GROUP, 4, *tile, dtype=BF),
        vmem(SLOTS * LANES, 2 * LANES, dtype=BF), vmem(SLOTS * LANES, 2 * LANES, dtype=BF),
        vmem(SLOTS * 2 * LANES, 2 * LANES, dtype=BF), vmem(LANES, LANES, dtype=BF),
        vmem(depth, 2 * LANES, LANES, dtype=BF),
        vmem(2, GROUP, 4, rows + 24, LANES), vmem(4, *tile),
        vmem(2, chips, 2, 8, LANES), vmem(chips, 2, 8, LANES),
        vmem(chips, 16, LANES, dtype=jnp.int16), vmem(chips, 16, LANES, dtype=jnp.int16),
        dma((6,)), dma((2,)), dma((2,)), dma((2, 2)), dma((2, 2)), dma((4,)), dma((4,)), dma, dma,
        dma((chips,)), dma((chips,)),
    ]
    inside = pl.BlockSpec(memory_space=pltpu.VMEM)
    anywhere = pl.BlockSpec(memory_space=pltpu.HBM)
    return pl.pallas_call(
        kernel,
        out_shape=jax.ShapeDtypeStruct((4, rows // ndep, LANES), F32),
        in_specs=[anywhere] * 6,
        out_specs=inside,
        scratch_shapes=scratch,
        compiler_params=pltpu.CompilerParams(
            collective_id=0, has_side_effects=True, vmem_limit_bytes=64 * 2 ** 20
        ),
    )(skew, frac, absorption, glow, density, temperature)


def solution(mesh):
    in_specs = (P("depth", None, "cols"), P("depth", None, "cols"), P(), P(), P(), P())
    out_specs = P(None, "depth", "cols")
    return jax.shard_map(
        on_device, mesh=mesh, in_specs=in_specs, out_specs=out_specs, check_vma=False
    )
```

```python
import functools
import math

import jax
import jax.numpy as jnp
from jax import lax
from jax.experimental import pallas as pl
from jax.experimental.pallas import tpu as pltpu
from jax.sharding import PartitionSpec as P

MESH = pl.DeviceIdType.MESH
BF = jnp.bfloat16
F32 = jnp.float32
I32 = jnp.int32
LANES = 128
PAD = 8
GROUP = 4
SLOT = 16
SLOTS = 8
UNROLL = 4
LEFT = 12
RIGHT = 4
NINTH = 14
SH = 8

ROOT = math.sqrt(0.7) * 2.0 ** -5
KX, KY, KZ = 0.48 * ROOT, 0.6 * ROOT, 0.64 * ROOT
AMBIENT = 0.3 * 2.0 ** -10
MAGIC0 = 1.5 * 2.0 ** 33
MAGIC1 = 1.5 * 2.0 ** 35
BIAS = 10240.0 * 1024.0
EXPO = -(2.0 ** -32) * math.log2(math.e)
CODES, SHIFT = 2600.0, 27500.0


def iota(shape, dim):
    return lax.broadcasted_iota(I32, shape, dim)


def table_words(absorption, glow):
    a = absorption.astype(F32) * 2.0 ** 22
    g = glow.astype(F32) * 2.0 ** 10
    w0 = (a - 10240.0) * 1024.0 + (g[0:1] - 612.0)
    w1 = g[1:2] * 4096.0 + g[2:3]
    parts = [w0[:, :LANES], w0[:, LANES:], w1[:, :LANES], w1[:, LANES:]]
    return [jnp.broadcast_to(p, (8, LANES)) for p in parts]


def encode(x):
    code = jnp.floor(jnp.log2(x) * CODES + (SHIFT + 0.5))
    return jnp.clip(code, -32767.0, 32767.0).astype(I32).astype(jnp.int16)


def decode(code):
    c = code.astype(I32).astype(F32)
    return jnp.where(c > -32767.0, jnp.exp2((c - SHIFT) * (1.0 / CODES)), 0.0)


def repeat(low, high, body, unroll):
    while (high - low) % unroll:
        unroll -= 1

    def step(n, _):
        for u in range(unroll):
            body(low + n * unroll + u, 0)
        return 0

    if unroll == high - low:
        step(0, 0)
    else:
        lax.fori_loop(0, (high - low) // unroll, step, 0)


def round_bf(x):
    return x.astype(BF).astype(F32)


def classify(d, up, down, zm, zp, gx, t, words):
    gy = down - up
    gz = zp - zm
    f = KX * gx + KY * gy + KZ * gz
    length = gx * gx + gy * gy + gz * gz + 1.0
    shade = AMBIENT + f * f * pl.reciprocal(length, approx=True)
    index = jnp.minimum((t * 128.0 - 64.0).astype(I32), 255)
    high = index >= LANES
    low_bits = index & (LANES - 1)

    def pick(word):
        table = jnp.concatenate([word] * (index.shape[0] // 8), 0)
        return jnp.take_along_axis(table, low_bits, axis=1, mode="promise_in_bounds")

    w0 = jnp.where(high, pick(words[1]), pick(words[0]))
    w1 = jnp.where(high, pick(words[3]), pick(words[2]))
    a = (w0 + MAGIC0) - (MAGIC0 - BIAS)
    g0 = (w0 - a) + (612.0 + BIAS)
    g1 = (w1 + MAGIC1) - MAGIC1
    g2 = w1 - g1
    alpha = 1.0 - jnp.exp2(a * (d * EXPO))
    p = alpha * shade * t
    return p * g0, (p * 2.0 ** -12) * g1, p * g2, alpha


def kernel(
    skew_in, frac_in, absorption, glow, dens, temp, out,
    skew, frac, absorb_v, glow_v,
    dv, tv, df, corner_out, corner_in,
    pd12, pd4, rd12, rd4, own_t, pt_r, pt_l, rt_l, rt_r,
    lf, rf, sd, dh, zph, zmh, th,
    gx_ref, vx, vh, part, sel_d, sel_t, sel_n, grad, wall, sheared, carry,
    hbuf, hrecv, comb, frecv,
    local_sem, plane_send, plane_recv, diag_send, diag_recv, pack_send, pack_recv, pair_send, pair_recv,
    out_send, out_recv,
):
    depth, rows, _ = tv.shape
    chips = comb.shape[0]
    col, dep = lax.axis_index("cols"), lax.axis_index("depth")
    ncol, ndep = lax.axis_size("cols"), lax.axis_size("depth")
    chip, core = dep // 2, dep % 2
    left, right = lax.rem(col + ncol - 1, ncol), lax.rem(col + 1, ncol)
    lower, upper = lax.rem(dep + ndep - 1, ndep), lax.rem(dep + 1, ndep)
    pair = dep + 1 - 2 * core
    base = dep * depth

    barrier = pltpu.get_barrier_semaphore()
    for c in (left, col, right):
        for e in (lower, dep, upper):
            if c is col and e is dep:
                continue
            pl.semaphore_signal(barrier, inc=1, device_id=(c, e), device_id_type=MESH)

    def greet(o, _):
        other = lax.rem(chip + o, chips) * 2 + core
        pl.semaphore_signal(barrier, inc=1, device_id=(col, other), device_id_type=MESH)
        return 0

    lax.fori_loop(1, chips, greet, 0)

    small = [
        pltpu.make_async_copy(a, b, local_sem.at[2 + n])
        for n, (a, b) in enumerate(
            ((skew_in, skew), (frac_in, frac), (absorption, absorb_v), (glow, glow_v))
        )
    ]
    for copy in small:
        copy.start()
    dens_in = pltpu.make_async_copy(dens, dv.at[pl.ds(1, depth)], local_sem.at[0])
    temp_in = pltpu.make_async_copy(temp, tv, local_sem.at[1])
    dens_in.start()
    temp_in.start()

    lane = iota((8, LANES), 1)
    kk, slot = lane % SLOT, lane // SLOT
    gk, gc = iota((LANES, LANES), 0), iota((LANES, LANES), 1)
    grad[...] = (jnp.where(gk == gc + 1, 1.0, 0.0) - jnp.where(gk == gc - 1, 1.0, 0.0)).astype(BF)
    far = 1 << 20
    for side, move in enumerate((LEFT, RIGHT)):
        at = slice(side * LANES, (side + 1) * LANES)
        off = (gk + move) % LANES
        keep = off < SLOT
        if side:
            keep = keep & (off != NINTH)
        to_d = jnp.where(keep, off - gc, far)
        if side == 0:
            to_t = jnp.where(gk == 0, LEFT - gc, jnp.where(gk == LANES - 1, RIGHT - 1 - gc, far))
            to_n = jnp.where(gk >= LANES - SH, gk - (LANES - SH) - gc, far)
        else:
            to_t = jnp.where(gk == SH, NINTH - gc, far)
            to_n = jnp.where(gk < SH, gk - gc, far)

        def build_sel(j, _):
            def put(ref, at_row, gap, lanes):
                row = pl.ds(pl.multiple_of(at_row * LANES, LANES), LANES)
                ref[row, at] = jnp.where(gap == -lanes, 1.0, 0.0).astype(BF)

            put(sel_d, j, to_d, j * SLOT)
            put(sel_t, j, to_t, j * SLOT)
            put(sel_n, 2 * j, to_n, j * SLOT)
            put(sel_n, 2 * j + 1, to_n, j * SLOT + SH)
            return 0

        repeat(0, SLOTS, build_sel, 2)

    def zero_df(z, _):
        df[z, 0:PAD, :] = jnp.zeros((PAD, LANES), F32)
        df[z, PAD + rows : PAD + rows + 8, :] = jnp.zeros((8, LANES), F32)
        return 0

    repeat(0, depth + 2, zero_df, 17)

    def zero_sheared(k, _):
        for s in range(2):
            for c in range(4):
                sheared[s, k, c, 0:PAD, :] = jnp.zeros((PAD, LANES), F32)
                sheared[s, k, c, PAD + rows : PAD + rows + 16, :] = jnp.zeros((16, LANES), F32)
        dh[k, 0:PAD, :] = jnp.zeros((PAD, LANES), F32)
        dh[k, PAD + rows : PAD + rows + 8, :] = jnp.zeros((8, LANES), F32)
        return 0

    lax.fori_loop(0, GROUP, zero_sheared, 0)

    for copy in small:
        copy.wait()
    def weights(row, z):
        part = jnp.full((8, LANES), frac[row, base + z], F32)
        return (1.0 - part).astype(BF).astype(F32), part.astype(BF).astype(F32)

    gap = jnp.where((gk > 0) & (gk < LANES - 1), gk - gc, 1000)
    hk, hc = iota((SLOT, LANES), 0), iota((SLOT, LANES), 1)

    def build_weights(z, _):
        s = skew[0, base + z]
        a0, a1 = weights(0, z)
        a0, a1 = a0[0:1], a1[0:1]
        wall[z, 0:LANES, :] = jnp.where(gap == s, a0, jnp.where(gap == s + 1, a1, 0.0)).astype(BF)
        wall[z, LANES:, :] = jnp.zeros((LANES, LANES), BF)
        use_right = (s >= 1) | ((s >= -1) & (hk < SLOT // 2))
        hcol = jnp.where(use_right, hk + (LANES - RIGHT), hk - LEFT)
        valid = (hcol <= 0) | (hcol >= LANES - 1)
        hgap = jnp.where(valid, hcol - hc, 1000)
        at = pl.ds(pl.multiple_of(LANES + (z // GROUP) * SLOT, SLOT), SLOT)
        wall[z, at, :] = jnp.where(hgap == s, a0, jnp.where(hgap == s + 1, a1, 0.0)).astype(BF)
        return 0

    repeat(0, depth, build_weights, 4)

    words = table_words(absorb_v[...].reshape(1, 2 * LANES), glow_v[...])
    def widen(z, _):
        df[z, PAD : PAD + rows, :] = dv[z].astype(F32)
        return 0

    def pack():
        def wide(ref, first):
            parts = [ref[pl.ds(first + GROUP * j, GROUP)] for j in range(SLOTS)]
            return jnp.concatenate([p.reshape(GROUP * rows, LANES) for p in parts], 1)

        both = jnp.dot(wide(dv, 1), sel_d[...], preferred_element_type=F32)
        more = jnp.dot(wide(tv, 0), sel_t[...], preferred_element_type=F32)
        for i in range(GROUP):
            at = slice(i * rows, (i + 1) * rows)
            pd12[i] = both[at, :LANES].astype(BF)
            pd4[i] = (both[at, LANES:] + more[at, LANES:]).astype(BF)
            own_t[i] = more[at, :LANES]

    def pack_narrow():
        parts = [
            jnp.concatenate([tv[GROUP * j + 2 * h + half] for h in range(2)], 0)
            for j in range(SLOTS) for half in range(2)
        ]
        both = jnp.dot(jnp.concatenate(parts, 1), sel_n[...], preferred_element_type=F32).astype(BF)
        for h in range(2):
            pt_r[h] = both[h * rows : (h + 1) * rows, :LANES]
            pt_l[h] = both[h * rows : (h + 1) * rows, LANES:]

    def fold(end, m, tile, source):
        folded = jnp.zeros((SLOT, LANES), F32)
        for k in range(rows // SLOT):
            part = tile[k * SLOT : (k + 1) * SLOT, :].astype(F32)
            folded = jnp.where(slot[0:1] == k, pltpu.roll(part, (k - source) % SLOTS * SLOT, 1), folded)
        corner_out[end, m] = folded.astype(BF)

    def unfold(end, m, target):
        part = corner_in[end, m].astype(F32)
        parts = [pltpu.roll(part, (target - k) % SLOTS * SLOT, 1) for k in range(rows // SLOT)]
        return jnp.concatenate(parts, 0)

    def send_pack(n, p, r, c):
        copy = pltpu.make_async_remote_copy(
            src_ref=p, dst_ref=r, send_sem=pack_send.at[n], recv_sem=pack_recv.at[n],
            device_id=(c, dep), device_id_type=MESH,
        )
        copy.start()
        return copy

    def shear_main(z):
        y = jnp.dot(
            vx[z].reshape(4 * rows, LANES), wall[z, 0:LANES, :], preferred_element_type=F32
        )
        part[z] = y.reshape(4, rows, LANES)

    def main_step(n, also=None, behind=True):
        places = [lax.rem(n * UNROLL + u + 1, depth) for u in range(UNROLL)]
        for u, z in enumerate(places):
            gx_ref[u] = jnp.dot(dv[z + 1], grad[...], preferred_element_type=F32)
        if also is not None:
            also()
        for u, z in enumerate(places):
            if behind:
                shear_main(lax.rem((n - 1) * UNROLL + u + 1, depth))
            for r in range(0, rows, 16):
                q = PAD + r
                values = classify(
                    df[z + 1, q : q + 16, :], df[z + 1, q - 1 : q + 15, :],
                    df[z + 1, q + 1 : q + 17, :],
                    df[z, q : q + 16, :], df[z + 2, q : q + 16, :],
                    gx_ref[u, r : r + 16, :], tv[z, r : r + 16, :].astype(F32), words,
                )
                for c in range(4):
                    vx[z, c, r : r + 16, :] = values[c].astype(BF)

    dens_in.wait()
    repeat(1, depth + 1, widen, 8)
    temp_in.wait()
    main_step(0, pack, False)

    pl.semaphore_wait(barrier, 8 + chips - 1)

    packs = [send_pack(0, pd12, rd12, right), send_pack(1, pd4, rd4, left)]
    planes, corners = [], []
    for n, (e, plane, end) in enumerate(((upper, depth - 1, 0), (lower, 0, 1))):
        planes.append(
            pltpu.make_async_remote_copy(
                src_ref=dens.at[plane], dst_ref=dv.at[end * (depth + 1)],
                send_sem=plane_send.at[n], recv_sem=plane_recv.at[n],
                device_id=(col, e), device_id_type=MESH,
            )
        )
        planes[-1].start()
        for m, (tiles, c) in enumerate(((pd12, right), (pd4, left))):
            fold(end, m, tiles.at[(GROUP - 1) * (1 - end)], (SLOTS - 1) * (1 - end))
            corners.append(
                pltpu.make_async_remote_copy(
                    src_ref=corner_out.at[end, m], dst_ref=corner_in.at[end, m],
                    send_sem=diag_send.at[n, m], recv_sem=diag_recv.at[n, m],
                    device_id=(c, e), device_id_type=MESH,
                )
            )
            corners[-1].start()
    main_step(1, pack_narrow)
    packs += [send_pack(2, pt_r, rt_l, right), send_pack(3, pt_l, rt_r, left)]
    blocks = depth // UNROLL
    lax.fori_loop(2, blocks - 1, lambda n, _: (main_step(n), 0)[1], 0)
    for copy in planes:
        copy.wait_recv()
    df[0, PAD : PAD + rows, :] = jnp.where(dep > 0, dv[0].astype(F32), 0.0)
    df[depth + 1, PAD : PAD + rows, :] = jnp.where(dep < ndep - 1, dv[depth + 1].astype(F32), 0.0)
    main_step(blocks - 1)
    for u in range(UNROLL):
        shear_main(((blocks - 1) * UNROLL + u + 1) % depth)

    for copy in packs + corners:
        copy.wait_recv()
    kk16, slot16 = kk[0:1], slot[0:1]
    has_left, has_right = col > 0, col < ncol - 1

    def windows(i, _):
        l = jnp.where(kk16 < LEFT, jnp.where(has_left, rd12[i].astype(F32), 0.0), pd12[i].astype(F32))
        r = jnp.where(kk16 < RIGHT, pd4[i].astype(F32), jnp.where(has_right, rd4[i].astype(F32), 0.0))
        lf[i + 1] = l
        rf[i + 1] = r
        return 0

    repeat(0, GROUP, windows, GROUP)
    for end, j, tile, other, shift, has in (
        (0, 0, 0, GROUP, SLOT, dep > 0),
        (1, SLOTS - 1, GROUP + 1, 1, LANES - SLOT, dep < ndep - 1),
    ):
        own = df[end * (depth + 1), PAD : PAD + rows, :]
        here = slot16 == j
        for m, (move, window, has_side) in enumerate(((LEFT, lf, has_left), (RIGHT, rf, has_right))):
            side = jnp.where(has_side & has, unfold(end, m, j), 0.0)
            mine = here & ((kk16 >= LEFT) if m == 0 else (kk16 < RIGHT))
            moved = jnp.where(here, side, pltpu.roll(window[other], shift, 1))
            window[tile] = jnp.where(mine, pltpu.roll(own, (j * SLOT + move) % LANES, 1), moved)

    def choose(i, _):
        sv = jnp.zeros((8, LANES), I32)
        for j in range(SLOTS):
            sv = jnp.where(slot == j, skew[0, base + GROUP * j + i], sv)
        use_right = ((sv >= 1) | ((sv >= -1) & (kk < SLOT // 2)))[0:1]
        center = jnp.where(use_right, rf[i + 1], lf[i + 1])
        dh[i, PAD : PAD + rows, :] = center
        sd[i] = center.astype(BF)
        zph[i] = jnp.where(use_right, rf[i + 2], lf[i + 2])
        zmh[i] = jnp.where(use_right, rf[i], lf[i])
        turn = jnp.where(lax.rem(i, 2) == 0, RIGHT, LANES - RIGHT)
        tl = pltpu.roll(rt_l[i // 2].astype(F32), turn, 1)
        tr = pltpu.roll(rt_r[i // 2].astype(F32), turn, 1)
        ninth = pltpu.roll(rd4[i].astype(F32), LANES - NINTH + LEFT, 1)
        tl = jnp.where(kk16 == LEFT, own_t[i], tl)
        tr = jnp.where(kk16 == RIGHT - 1, own_t[i], jnp.where(kk16 == LEFT, ninth, tr))
        th[i] = jnp.where(use_right, tr, tl)
        return 0

    repeat(0, GROUP, choose, GROUP)

    def halo_step(n, _):
        for u in range(2):
            gx_ref[u] = jnp.dot(sd[2 * n + u], grad[...], preferred_element_type=F32)
        for u in range(2):
            i = 2 * n + u
            for r in range(0, rows, 16):
                q = PAD + r
                values = classify(
                    dh[i, q : q + 16, :], dh[i, q - 1 : q + 15, :], dh[i, q + 1 : q + 17, :],
                    zmh[i, r : r + 16, :], zph[i, r : r + 16, :],
                    gx_ref[u, r : r + 16, :], th[i, r : r + 16, :], words,
                )
                for c in range(4):
                    vh[i, c, r : r + 16, :] = values[c].astype(BF)
        return 0

    lax.fori_loop(0, GROUP // 2, halo_step, 0)

    back = skew[0, 0] > 0

    def eye(step):
        return jnp.where(back, depth - 1 - step, step)

    def shear(g, place, quarters=range(GROUP)):
        for i in quarters:
            z = eye(g * GROUP + i)
            y = jnp.dot(
                vh[lax.rem(z, GROUP)].reshape(4 * rows, LANES), wall[z, LANES:, :],
                preferred_element_type=F32,
            )
            y = round_bf(y + part[z].reshape(4 * rows, LANES))
            for c in range(4):
                sheared[place, i, c, PAD : PAD + rows, :] = y[c * rows : (c + 1) * rows]

    carry[0:3] = jnp.zeros((3, rows, LANES), F32)
    carry[3] = jnp.ones((rows, LANES), F32)

    def composite(g, place, quarters=range(GROUP)):
        taps = []
        for i in range(GROUP):
            z = eye(g * GROUP + i)
            taps.append((skew[1, base + z], weights(1, z)))
        tiles = rows // (8 * GROUP) if rows >= 8 * GROUP else rows // 8
        for r in [8 * (q * tiles + k) for q in quarters for k in range(tiles) if 8 * (q * tiles + k) < rows]:
            acc = [carry[c, r : r + 8, :] for c in range(4)]
            for i in range(GROUP):
                t, (b0, b1) = taps[i]
                sample = [
                    b0 * sheared[place, i, c, pl.ds(PAD + r + t, 8), :]
                    + b1 * sheared[place, i, c, pl.ds(PAD + r + t + 1, 8), :]
                    for c in range(4)
                ]
                keep = 1.0 - sample[3]
                for c in range(3):
                    acc[c] = acc[c] + acc[3] * sample[c]
                acc[3] = acc[3] * keep
            for c in range(4):
                carry[c, r : r + 8, :] = acc[c]

    groups = depth // GROUP
    shear(0, 0)

    def fused(g, _):
        for q in range(GROUP):
            shear(g, lax.rem(g, 2), (q,))
            composite(g - 1, lax.rem(g + 1, 2), (q,))
        return 0

    lax.fori_loop(1, groups, fused, 0)
    composite(groups - 1, (groups - 1) % 2)

    top = iota((8, LANES), 0) < 4

    def halves(k, _):
        at = pl.ds(pl.multiple_of(k * 8, 8), 8)
        v = [carry[c, at, :] for c in range(4)]
        for p in range(2):
            hbuf[0, k, p] = jnp.where(top, v[2 * p], pltpu.roll(v[2 * p + 1], 4, 0))
            hbuf[1, k, p] = jnp.where(top, pltpu.roll(v[2 * p], 4, 0), v[2 * p + 1])
        return 0

    repeat(0, chips, halves, chips)
    swap = pltpu.make_async_remote_copy(
        src_ref=hbuf.at[1 - core], dst_ref=hrecv, send_sem=pair_send, recv_sem=pair_recv,
        device_id=(col, pair), device_id_type=MESH,
    )
    swap.start()
    swap.wait_recv()
    mine_near = (core == 0) != back

    def join(k, _):
        mine = [hbuf[core, k, p] for p in range(2)]
        other = [hrecv[k, p] for p in range(2)]
        near = [jnp.where(mine_near, mine[p], other[p]) for p in range(2)]
        far = [jnp.where(mine_near, other[p], mine[p]) for p in range(2)]
        through = jnp.where(top, pltpu.roll(near[1], 4, 0), near[1])
        first = near[0] + through * far[0]
        second = jnp.where(top, near[1] + through * far[1], 1.0 - through * far[1])
        comb[k] = encode(jnp.concatenate([first, second], 0))
        return 0

    repeat(0, chips, join, chips)

    def out_copy(o):
        to = lax.rem(chip + o, chips)
        return pltpu.make_async_remote_copy(
            src_ref=comb.at[to], dst_ref=frecv.at[chip],
            send_sem=out_send.at[o], recv_sem=out_recv.at[o],
            device_id=(col, to * 2 + core), device_id_type=MESH,
        )

    for n in range(chips - 1):
        out_copy(chips // 2 + (n + 1) // 2 * (1 if n % 2 == 0 else -1)).start()
    frecv[chip] = comb[chip]

    def arrive(o, _):
        pltpu.make_async_remote_copy(
            src_ref=comb.at[chip], dst_ref=frecv.at[lax.rem(chip + chips - o, chips)],
            send_sem=out_send.at[o], recv_sem=out_recv.at[o],
            device_id=(col, dep), device_id_type=MESH,
        ).wait_recv()
        return 0

    lax.fori_loop(1, chips, arrive, 0)

    def final(n, state):
        s0, s1, through = state
        k = jnp.where(back, chips - 1 - n, n)
        v = decode(frecv[k])
        v0, v1 = v[:8], v[8:]
        s0 = s0 + through * v0
        s1 = s1 + through * v1
        through = through * (1.0 - jnp.where(top, pltpu.roll(v1, 4, 0), v1))
        return s0, s1, through

    zero = jnp.zeros((8, LANES), F32)
    state = (zero, zero, zero + 1.0)
    for n in range(chips):
        state = final(n, state)
    s0, s1, _ = state
    out[0] = s0[0:4]
    out[1] = s0[4:8]
    out[2] = s1[0:4]
    out[3] = s1[4:8]

    for copy in planes + corners + packs + [swap]:
        copy.wait_send()
    lax.fori_loop(1, chips, lambda o, _: (out_copy(o).wait_send(), 0)[1], 0)


def on_device(density, temperature, absorption, glow, skew, frac):
    depth, rows, _ = density.shape
    ndep = lax.axis_size("depth")
    chips = ndep // 2
    vmem = lambda *shape, dtype=F32: pltpu.VMEM(shape, dtype)
    tile = (rows, LANES)
    dma = pltpu.SemaphoreType.DMA
    scratch = [
        pltpu.SMEM(skew.shape, I32), pltpu.SMEM(frac.shape, F32),
        vmem(2 * LANES, dtype=BF), vmem(3, 2 * LANES, dtype=BF),
        vmem(depth + 2, *tile, dtype=BF), vmem(depth, *tile, dtype=BF),
        vmem(depth + 2, rows + 16, LANES), vmem(2, 2, SLOT, LANES, dtype=BF), vmem(2, 2, SLOT, LANES, dtype=BF),
    ]
    scratch += [vmem(GROUP, *tile, dtype=BF)] * 4 + [vmem(GROUP, *tile)]
    scratch += [vmem(GROUP // 2, *tile, dtype=BF)] * 4
    scratch += [
        vmem(GROUP + 2, *tile), vmem(GROUP + 2, *tile), vmem(GROUP, *tile, dtype=BF),
        vmem(GROUP, rows + 16, LANES), vmem(GROUP, *tile), vmem(GROUP, *tile), vmem(GROUP, *tile),
        vmem(UNROLL, *tile), vmem(depth, 4, *tile, dtype=BF), vmem(GROUP, 4, *tile, dtype=BF), vmem(depth, 4, *tile),
        vmem(SLOTS * LANES, 2 * LANES, dtype=BF), vmem(SLOTS * LANES, 2 * LANES, dtype=BF),
        vmem(SLOTS * 2 * LANES, 2 * LANES, dtype=BF), vmem(LANES, LANES, dtype=BF),
        vmem(depth, 2 * LANES, LANES, dtype=BF),
        vmem(2, GROUP, 4, rows + 24, LANES), vmem(4, *tile),
        vmem(2, chips, 2, 8, LANES), vmem(chips, 2, 8, LANES),
        vmem(chips, 16, LANES, dtype=jnp.int16), vmem(chips, 16, LANES, dtype=jnp.int16),
        dma((6,)), dma((2,)), dma((2,)), dma((2, 2)), dma((2, 2)), dma((4,)), dma((4,)), dma, dma,
        dma((chips,)), dma((chips,)),
    ]
    inside = pl.BlockSpec(memory_space=pltpu.VMEM)
    anywhere = pl.BlockSpec(memory_space=pltpu.HBM)
    return pl.pallas_call(
        kernel,
        out_shape=jax.ShapeDtypeStruct((4, rows // ndep, LANES), F32),
        in_specs=[anywhere] * 6,
        out_specs=inside,
        scratch_shapes=scratch,
        compiler_params=pltpu.CompilerParams(
            collective_id=0, has_side_effects=True, vmem_limit_bytes=64 * 2 ** 20
        ),
    )(skew, frac, absorption, glow, density, temperature)


def solution(mesh):
    in_specs = (P("depth", None, "cols"), P("depth", None, "cols"), P(), P(), P(), P())
    out_specs = P(None, "depth", "cols")
    return jax.shard_map(
        on_device, mesh=mesh, in_specs=in_specs, out_specs=out_specs, check_vma=False
    )
```

```python
import functools
import math

import jax
import jax.numpy as jnp
from jax import lax
from jax.experimental import pallas as pl
from jax.experimental.pallas import tpu as pltpu
from jax.sharding import PartitionSpec as P

MESH = pl.DeviceIdType.MESH
BF = jnp.bfloat16
F32 = jnp.float32
I32 = jnp.int32
LANES = 128
PAD = 8
GROUP = 4
SLOT = 16
SLOTS = 8
UNROLL = 4
LEFT = 12
RIGHT = 4
NINTH = 14
SH = 8

ROOT = math.sqrt(0.7) * 2.0 ** -5
KX, KY, KZ = 0.48 * ROOT, 0.6 * ROOT, 0.64 * ROOT
AMBIENT = 0.3 * 2.0 ** -10
MAGIC0 = 1.5 * 2.0 ** 33
MAGIC1 = 1.5 * 2.0 ** 35
BIAS = 10240.0 * 1024.0
EXPO = -(2.0 ** -32) * math.log2(math.e)
CODES, SHIFT = 2600.0, 27500.0


def iota(shape, dim):
    return lax.broadcasted_iota(I32, shape, dim)


def table_words(absorption, glow):
    a = absorption.astype(F32) * 2.0 ** 22
    g = glow.astype(F32) * 2.0 ** 10
    w0 = (a - 10240.0) * 1024.0 + (g[0:1] - 612.0)
    w1 = g[1:2] * 4096.0 + g[2:3]
    parts = [w0[:, :LANES], w0[:, LANES:], w1[:, :LANES], w1[:, LANES:]]
    return [jnp.broadcast_to(p, (8, LANES)) for p in parts]


def encode(x):
    code = jnp.floor(jnp.log2(x) * CODES + (SHIFT + 0.5))
    return jnp.clip(code, -32767.0, 32767.0).astype(I32).astype(jnp.int16)


def decode(code):
    c = code.astype(I32).astype(F32)
    return jnp.where(c > -32767.0, jnp.exp2((c - SHIFT) * (1.0 / CODES)), 0.0)


def repeat(low, high, body, unroll):
    while (high - low) % unroll:
        unroll -= 1

    def step(n, _):
        for u in range(unroll):
            body(low + n * unroll + u, 0)
        return 0

    if unroll == high - low:
        step(0, 0)
    else:
        lax.fori_loop(0, (high - low) // unroll, step, 0)


def round_bf(x):
    return x.astype(BF).astype(F32)


def classify(d, up, down, zm, zp, gx, t, words):
    gy = down - up
    gz = zp - zm
    f = KX * gx + KY * gy + KZ * gz
    length = gx * gx + gy * gy + gz * gz + 1.0
    shade = AMBIENT + f * f * pl.reciprocal(length, approx=True)
    index = jnp.minimum((t * 128.0 - 64.0).astype(I32), 255)
    high = index >= LANES
    low_bits = index & (LANES - 1)

    def pick(word):
        table = jnp.concatenate([word] * (index.shape[0] // 8), 0)
        return jnp.take_along_axis(table, low_bits, axis=1, mode="promise_in_bounds")

    w0 = jnp.where(high, pick(words[1]), pick(words[0]))
    w1 = jnp.where(high, pick(words[3]), pick(words[2]))
    a = (w0 + MAGIC0) - (MAGIC0 - BIAS)
    g0 = (w0 - a) + (612.0 + BIAS)
    g1 = (w1 + MAGIC1) - MAGIC1
    g2 = w1 - g1
    alpha = 1.0 - jnp.exp2(a * (d * EXPO))
    p = alpha * shade * t
    return p * g0, (p * 2.0 ** -12) * g1, p * g2, alpha


def kernel(
    skew_in, frac_in, absorption, glow, dens, temp, out,
    skew, frac, absorb_v, glow_v,
    dv, tv, df, corner_out, corner_in,
    pd12, pd4, rd12, rd4, own_t, pt_r, pt_l, rt_l, rt_r,
    lf, rf, sd, dh, zph, zmh, th,
    gx_ref, vx, vh, part, sel_d, sel_t, sel_n, grad, wall, sheared, carry,
    hbuf, hrecv, comb, frecv,
    local_sem, plane_send, plane_recv, diag_send, diag_recv, pack_send, pack_recv, pair_send, pair_recv,
    out_send, out_recv,
):
    depth, rows, _ = tv.shape
    chips = comb.shape[0]
    col, dep = lax.axis_index("cols"), lax.axis_index("depth")
    ncol, ndep = lax.axis_size("cols"), lax.axis_size("depth")
    chip, core = dep // 2, dep % 2
    left, right = lax.rem(col + ncol - 1, ncol), lax.rem(col + 1, ncol)
    lower, upper = lax.rem(dep + ndep - 1, ndep), lax.rem(dep + 1, ndep)
    pair = dep + 1 - 2 * core
    base = dep * depth

    barrier = pltpu.get_barrier_semaphore()
    for c in (left, col, right):
        for e in (lower, dep, upper):
            if c is col and e is dep:
                continue
            pl.semaphore_signal(barrier, inc=1, device_id=(c, e), device_id_type=MESH)

    def greet(o, _):
        other = lax.rem(chip + o, chips) * 2 + core
        pl.semaphore_signal(barrier, inc=1, device_id=(col, other), device_id_type=MESH)
        return 0

    lax.fori_loop(1, chips, greet, 0)

    small = [
        pltpu.make_async_copy(a, b, local_sem.at[2 + n])
        for n, (a, b) in enumerate(
            ((skew_in, skew), (frac_in, frac), (absorption, absorb_v), (glow, glow_v))
        )
    ]
    for copy in small:
        copy.start()
    dens_in = pltpu.make_async_copy(dens, dv.at[pl.ds(1, depth)], local_sem.at[0])
    temp_in = pltpu.make_async_copy(temp, tv, local_sem.at[1])
    dens_in.start()
    temp_in.start()

    lane = iota((8, LANES), 1)
    kk, slot = lane % SLOT, lane // SLOT
    gk, gc = iota((LANES, LANES), 0), iota((LANES, LANES), 1)
    grad[...] = (jnp.where(gk == gc + 1, 1.0, 0.0) - jnp.where(gk == gc - 1, 1.0, 0.0)).astype(BF)
    far = 1 << 20
    for side, move in enumerate((LEFT, RIGHT)):
        at = slice(side * LANES, (side + 1) * LANES)
        off = (gk + move) % LANES
        keep = off < SLOT
        if side:
            keep = keep & (off != NINTH)
        to_d = jnp.where(keep, off - gc, far)
        if side == 0:
            to_t = jnp.where(gk == 0, LEFT - gc, jnp.where(gk == LANES - 1, RIGHT - 1 - gc, far))
            to_n = jnp.where(gk >= LANES - SH, gk - (LANES - SH) - gc, far)
        else:
            to_t = jnp.where(gk == SH, NINTH - gc, far)
            to_n = jnp.where(gk < SH, gk - gc, far)

        def build_sel(j, _):
            def put(ref, at_row, gap, lanes):
                row = pl.ds(pl.multiple_of(at_row * LANES, LANES), LANES)
                ref[row, at] = jnp.where(gap == -lanes, 1.0, 0.0).astype(BF)

            put(sel_d, j, to_d, j * SLOT)
            put(sel_t, j, to_t, j * SLOT)
            put(sel_n, 2 * j, to_n, j * SLOT)
            put(sel_n, 2 * j + 1, to_n, j * SLOT + SH)
            return 0

        repeat(0, SLOTS, build_sel, 2)

    def zero_df(z, _):
        df[z, 0:PAD, :] = jnp.zeros((PAD, LANES), F32)
        df[z, PAD + rows : PAD + rows + 8, :] = jnp.zeros((8, LANES), F32)
        return 0

    repeat(0, depth + 2, zero_df, 17)

    def zero_sheared(k, _):
        for s in range(2):
            for c in range(4):
                sheared[s, k, c, 0:PAD, :] = jnp.zeros((PAD, LANES), F32)
                sheared[s, k, c, PAD + rows : PAD + rows + 16, :] = jnp.zeros((16, LANES), F32)
        dh[k, 0:PAD, :] = jnp.zeros((PAD, LANES), F32)
        dh[k, PAD + rows : PAD + rows + 8, :] = jnp.zeros((8, LANES), F32)
        return 0

    lax.fori_loop(0, GROUP, zero_sheared, 0)

    for copy in small:
        copy.wait()
    def weights(row, z):
        part = jnp.full((8, LANES), frac[row, base + z], F32)
        return (1.0 - part).astype(BF).astype(F32), part.astype(BF).astype(F32)

    gap = jnp.where((gk > 0) & (gk < LANES - 1), gk - gc, 1000)
    hk, hc = iota((SLOT, LANES), 0), iota((SLOT, LANES), 1)

    def build_weights(z, _):
        s = skew[0, base + z]
        a0, a1 = weights(0, z)
        a0, a1 = a0[0:1], a1[0:1]
        wall[z, 0:LANES, :] = jnp.where(gap == s, a0, jnp.where(gap == s + 1, a1, 0.0)).astype(BF)
        wall[z, LANES:, :] = jnp.zeros((LANES, LANES), BF)
        use_right = (s >= 1) | ((s >= -1) & (hk < SLOT // 2))
        hcol = jnp.where(use_right, hk + (LANES - RIGHT), hk - LEFT)
        valid = (hcol <= 0) | (hcol >= LANES - 1)
        hgap = jnp.where(valid, hcol - hc, 1000)
        at = pl.ds(pl.multiple_of(LANES + (z // GROUP) * SLOT, SLOT), SLOT)
        wall[z, at, :] = jnp.where(hgap == s, a0, jnp.where(hgap == s + 1, a1, 0.0)).astype(BF)
        return 0

    repeat(0, depth, build_weights, 4)

    words = table_words(absorb_v[...].reshape(1, 2 * LANES), glow_v[...])
    def widen(z, _):
        df[z, PAD : PAD + rows, :] = dv[z].astype(F32)
        return 0

    def pack():
        def wide(ref, first):
            parts = [ref[pl.ds(first + GROUP * j, GROUP)] for j in range(SLOTS)]
            return jnp.concatenate([p.reshape(GROUP * rows, LANES) for p in parts], 1)

        both = jnp.dot(wide(dv, 1), sel_d[...], preferred_element_type=F32)
        more = jnp.dot(wide(tv, 0), sel_t[...], preferred_element_type=F32)
        for i in range(GROUP):
            at = slice(i * rows, (i + 1) * rows)
            pd12[i] = both[at, :LANES].astype(BF)
            pd4[i] = (both[at, LANES:] + more[at, LANES:]).astype(BF)
            own_t[i] = more[at, :LANES]

    def pack_narrow():
        parts = [
            jnp.concatenate([tv[GROUP * j + 2 * h + half] for h in range(2)], 0)
            for j in range(SLOTS) for half in range(2)
        ]
        both = jnp.dot(jnp.concatenate(parts, 1), sel_n[...], preferred_element_type=F32).astype(BF)
        for h in range(2):
            pt_r[h] = both[h * rows : (h + 1) * rows, :LANES]
            pt_l[h] = both[h * rows : (h + 1) * rows, LANES:]

    def fold(end, m, tile, source):
        folded = jnp.zeros((SLOT, LANES), F32)
        for k in range(rows // SLOT):
            part = tile[k * SLOT : (k + 1) * SLOT, :].astype(F32)
            folded = jnp.where(slot[0:1] == k, pltpu.roll(part, (k - source) % SLOTS * SLOT, 1), folded)
        corner_out[end, m] = folded.astype(BF)

    def unfold(end, m, target):
        part = corner_in[end, m].astype(F32)
        parts = [pltpu.roll(part, (target - k) % SLOTS * SLOT, 1) for k in range(rows // SLOT)]
        return jnp.concatenate(parts, 0)

    def send_pack(n, p, r, c):
        copy = pltpu.make_async_remote_copy(
            src_ref=p, dst_ref=r, send_sem=pack_send.at[n], recv_sem=pack_recv.at[n],
            device_id=(c, dep), device_id_type=MESH,
        )
        copy.start()
        return copy

    def shear_main(z):
        y = jnp.dot(
            vx[z].reshape(4 * rows, LANES), wall[z, 0:LANES, :], preferred_element_type=F32
        )
        part[z] = y.reshape(4, rows, LANES)

    def main_step(n, also=None, behind=True):
        places = [lax.rem(n * UNROLL + u + 1, depth) for u in range(UNROLL)]
        for u, z in enumerate(places):
            gx_ref[u] = jnp.dot(dv[z + 1], grad[...], preferred_element_type=F32)
        if also is not None:
            also()
        for u, z in enumerate(places):
            if behind:
                shear_main(lax.rem((n - 1) * UNROLL + u + 1, depth))
            for r in range(0, rows, 16):
                q = PAD + r
                values = classify(
                    df[z + 1, q : q + 16, :], df[z + 1, q - 1 : q + 15, :],
                    df[z + 1, q + 1 : q + 17, :],
                    df[z, q : q + 16, :], df[z + 2, q : q + 16, :],
                    gx_ref[u, r : r + 16, :], tv[z, r : r + 16, :].astype(F32), words,
                )
                for c in range(4):
                    vx[z, c, r : r + 16, :] = values[c].astype(BF)

    dens_in.wait()
    temp_in.wait()
    repeat(1, depth + 1, widen, depth)
    pack()

    pl.semaphore_wait(barrier, 8 + chips - 1)

    packs = [send_pack(0, pd12, rd12, right), send_pack(1, pd4, rd4, left)]
    planes, corners = [], []
    for n, (e, plane, end) in enumerate(((upper, depth - 1, 0), (lower, 0, 1))):
        planes.append(
            pltpu.make_async_remote_copy(
                src_ref=dens.at[plane], dst_ref=dv.at[end * (depth + 1)],
                send_sem=plane_send.at[n], recv_sem=plane_recv.at[n],
                device_id=(col, e), device_id_type=MESH,
            )
        )
        planes[-1].start()
        for m, (tiles, c) in enumerate(((pd12, right), (pd4, left))):
            fold(end, m, tiles.at[(GROUP - 1) * (1 - end)], (SLOTS - 1) * (1 - end))
            corners.append(
                pltpu.make_async_remote_copy(
                    src_ref=corner_out.at[end, m], dst_ref=corner_in.at[end, m],
                    send_sem=diag_send.at[n, m], recv_sem=diag_recv.at[n, m],
                    device_id=(c, e), device_id_type=MESH,
                )
            )
            corners[-1].start()
    main_step(0, pack_narrow, False)
    packs += [send_pack(2, pt_r, rt_l, right), send_pack(3, pt_l, rt_r, left)]
    blocks = depth // UNROLL
    lax.fori_loop(1, blocks - 1, lambda n, _: (main_step(n), 0)[1], 0)
    for copy in planes:
        copy.wait_recv()
    df[0, PAD : PAD + rows, :] = jnp.where(dep > 0, dv[0].astype(F32), 0.0)
    df[depth + 1, PAD : PAD + rows, :] = jnp.where(dep < ndep - 1, dv[depth + 1].astype(F32), 0.0)
    main_step(blocks - 1)
    for u in range(UNROLL):
        shear_main(((blocks - 1) * UNROLL + u + 1) % depth)

    for copy in packs + corners:
        copy.wait_recv()
    kk16, slot16 = kk[0:1], slot[0:1]
    has_left, has_right = col > 0, col < ncol - 1

    def windows(i, _):
        l = jnp.where(kk16 < LEFT, jnp.where(has_left, rd12[i].astype(F32), 0.0), pd12[i].astype(F32))
        r = jnp.where(kk16 < RIGHT, pd4[i].astype(F32), jnp.where(has_right, rd4[i].astype(F32), 0.0))
        lf[i + 1] = l
        rf[i + 1] = r
        return 0

    repeat(0, GROUP, windows, GROUP)
    for end, j, tile, other, shift, has in (
        (0, 0, 0, GROUP, SLOT, dep > 0),
        (1, SLOTS - 1, GROUP + 1, 1, LANES - SLOT, dep < ndep - 1),
    ):
        own = df[end * (depth + 1), PAD : PAD + rows, :]
        here = slot16 == j
        for m, (move, window, has_side) in enumerate(((LEFT, lf, has_left), (RIGHT, rf, has_right))):
            side = jnp.where(has_side & has, unfold(end, m, j), 0.0)
            mine = here & ((kk16 >= LEFT) if m == 0 else (kk16 < RIGHT))
            moved = jnp.where(here, side, pltpu.roll(window[other], shift, 1))
            window[tile] = jnp.where(mine, pltpu.roll(own, (j * SLOT + move) % LANES, 1), moved)

    def choose(i, _):
        sv = jnp.zeros((8, LANES), I32)
        for j in range(SLOTS):
            sv = jnp.where(slot == j, skew[0, base + GROUP * j + i], sv)
        use_right = ((sv >= 1) | ((sv >= -1) & (kk < SLOT // 2)))[0:1]
        center = jnp.where(use_right, rf[i + 1], lf[i + 1])
        dh[i, PAD : PAD + rows, :] = center
        sd[i] = center.astype(BF)
        zph[i] = jnp.where(use_right, rf[i + 2], lf[i + 2])
        zmh[i] = jnp.where(use_right, rf[i], lf[i])
        turn = jnp.where(lax.rem(i, 2) == 0, RIGHT, LANES - RIGHT)
        tl = pltpu.roll(rt_l[i // 2].astype(F32), turn, 1)
        tr = pltpu.roll(rt_r[i // 2].astype(F32), turn, 1)
        ninth = pltpu.roll(rd4[i].astype(F32), LANES - NINTH + LEFT, 1)
        tl = jnp.where(kk16 == LEFT, own_t[i], tl)
        tr = jnp.where(kk16 == RIGHT - 1, own_t[i], jnp.where(kk16 == LEFT, ninth, tr))
        th[i] = jnp.where(use_right, tr, tl)
        return 0

    repeat(0, GROUP, choose, GROUP)

    def halo_step(n, _):
        for u in range(2):
            gx_ref[u] = jnp.dot(sd[2 * n + u], grad[...], preferred_element_type=F32)
        for u in range(2):
            i = 2 * n + u
            for r in range(0, rows, 16):
                q = PAD + r
                values = classify(
                    dh[i, q : q + 16, :], dh[i, q - 1 : q + 15, :], dh[i, q + 1 : q + 17, :],
                    zmh[i, r : r + 16, :], zph[i, r : r + 16, :],
                    gx_ref[u, r : r + 16, :], th[i, r : r + 16, :], words,
                )
                for c in range(4):
                    vh[i, c, r : r + 16, :] = values[c].astype(BF)
        return 0

    lax.fori_loop(0, GROUP // 2, halo_step, 0)

    back = skew[0, 0] > 0

    def eye(step):
        return jnp.where(back, depth - 1 - step, step)

    def shear(g, place, quarters=range(GROUP)):
        for i in quarters:
            z = eye(g * GROUP + i)
            y = jnp.dot(
                vh[lax.rem(z, GROUP)].reshape(4 * rows, LANES), wall[z, LANES:, :],
                preferred_element_type=F32,
            )
            y = round_bf(y + part[z].reshape(4 * rows, LANES))
            for c in range(4):
                sheared[place, i, c, PAD : PAD + rows, :] = y[c * rows : (c + 1) * rows]

    carry[0:3] = jnp.zeros((3, rows, LANES), F32)
    carry[3] = jnp.ones((rows, LANES), F32)

    def composite(g, place, quarters=range(GROUP)):
        taps = []
        for i in range(GROUP):
            z = eye(g * GROUP + i)
            taps.append((skew[1, base + z], weights(1, z)))
        tiles = rows // (8 * GROUP) if rows >= 8 * GROUP else rows // 8
        for r in [8 * (q * tiles + k) for q in quarters for k in range(tiles) if 8 * (q * tiles + k) < rows]:
            acc = [carry[c, r : r + 8, :] for c in range(4)]
            for i in range(GROUP):
                t, (b0, b1) = taps[i]
                sample = [
                    b0 * sheared[place, i, c, pl.ds(PAD + r + t, 8), :]
                    + b1 * sheared[place, i, c, pl.ds(PAD + r + t + 1, 8), :]
                    for c in range(4)
                ]
                keep = 1.0 - sample[3]
                for c in range(3):
                    acc[c] = acc[c] + acc[3] * sample[c]
                acc[3] = acc[3] * keep
            for c in range(4):
                carry[c, r : r + 8, :] = acc[c]

    groups = depth // GROUP
    shear(0, 0)

    def fused(g, _):
        for q in range(GROUP):
            shear(g, lax.rem(g, 2), (q,))
            composite(g - 1, lax.rem(g + 1, 2), (q,))
        return 0

    lax.fori_loop(1, groups, fused, 0)
    composite(groups - 1, (groups - 1) % 2)

    top = iota((8, LANES), 0) < 4

    def halves(k, _):
        at = pl.ds(pl.multiple_of(k * 8, 8), 8)
        v = [carry[c, at, :] for c in range(4)]
        for p in range(2):
            hbuf[0, k, p] = jnp.where(top, v[2 * p], pltpu.roll(v[2 * p + 1], 4, 0))
            hbuf[1, k, p] = jnp.where(top, pltpu.roll(v[2 * p], 4, 0), v[2 * p + 1])
        return 0

    repeat(0, chips, halves, chips)
    swap = pltpu.make_async_remote_copy(
        src_ref=hbuf.at[1 - core], dst_ref=hrecv, send_sem=pair_send, recv_sem=pair_recv,
        device_id=(col, pair), device_id_type=MESH,
    )
    swap.start()
    swap.wait_recv()
    mine_near = (core == 0) != back

    def join(k, _):
        mine = [hbuf[core, k, p] for p in range(2)]
        other = [hrecv[k, p] for p in range(2)]
        near = [jnp.where(mine_near, mine[p], other[p]) for p in range(2)]
        far = [jnp.where(mine_near, other[p], mine[p]) for p in range(2)]
        through = jnp.where(top, pltpu.roll(near[1], 4, 0), near[1])
        first = near[0] + through * far[0]
        second = jnp.where(top, near[1] + through * far[1], 1.0 - through * far[1])
        comb[k] = encode(jnp.concatenate([first, second], 0))
        return 0

    repeat(0, chips, join, chips)

    def out_copy(o):
        to = lax.rem(chip + o, chips)
        return pltpu.make_async_remote_copy(
            src_ref=comb.at[to], dst_ref=frecv.at[chip],
            send_sem=out_send.at[o], recv_sem=out_recv.at[o],
            device_id=(col, to * 2 + core), device_id_type=MESH,
        )

    for n in range(chips - 1):
        out_copy(chips // 2 + (n + 1) // 2 * (1 if n % 2 == 0 else -1)).start()
    frecv[chip] = comb[chip]

    def arrive(o, _):
        pltpu.make_async_remote_copy(
            src_ref=comb.at[chip], dst_ref=frecv.at[lax.rem(chip + chips - o, chips)],
            send_sem=out_send.at[o], recv_sem=out_recv.at[o],
            device_id=(col, dep), device_id_type=MESH,
        ).wait_recv()
        return 0

    lax.fori_loop(1, chips, arrive, 0)

    def final(n, state):
        s0, s1, through = state
        k = jnp.where(back, chips - 1 - n, n)
        v = decode(frecv[k])
        v0, v1 = v[:8], v[8:]
        s0 = s0 + through * v0
        s1 = s1 + through * v1
        through = through * (1.0 - jnp.where(top, pltpu.roll(v1, 4, 0), v1))
        return s0, s1, through

    zero = jnp.zeros((8, LANES), F32)
    state = (zero, zero, zero + 1.0)
    for n in range(chips):
        state = final(n, state)
    s0, s1, _ = state
    out[0] = s0[0:4]
    out[1] = s0[4:8]
    out[2] = s1[0:4]
    out[3] = s1[4:8]

    for copy in planes + corners + packs + [swap]:
        copy.wait_send()
    lax.fori_loop(1, chips, lambda o, _: (out_copy(o).wait_send(), 0)[1], 0)


def on_device(density, temperature, absorption, glow, skew, frac):
    depth, rows, _ = density.shape
    ndep = lax.axis_size("depth")
    chips = ndep // 2
    vmem = lambda *shape, dtype=F32: pltpu.VMEM(shape, dtype)
    tile = (rows, LANES)
    dma = pltpu.SemaphoreType.DMA
    scratch = [
        pltpu.SMEM(skew.shape, I32), pltpu.SMEM(frac.shape, F32),
        vmem(2 * LANES, dtype=BF), vmem(3, 2 * LANES, dtype=BF),
        vmem(depth + 2, *tile, dtype=BF), vmem(depth, *tile, dtype=BF),
        vmem(depth + 2, rows + 16, LANES), vmem(2, 2, SLOT, LANES, dtype=BF), vmem(2, 2, SLOT, LANES, dtype=BF),
    ]
    scratch += [vmem(GROUP, *tile, dtype=BF)] * 4 + [vmem(GROUP, *tile)]
    scratch += [vmem(GROUP // 2, *tile, dtype=BF)] * 4
    scratch += [
        vmem(GROUP + 2, *tile), vmem(GROUP + 2, *tile), vmem(GROUP, *tile, dtype=BF),
        vmem(GROUP, rows + 16, LANES), vmem(GROUP, *tile), vmem(GROUP, *tile), vmem(GROUP, *tile),
        vmem(UNROLL, *tile), vmem(depth, 4, *tile, dtype=BF), vmem(GROUP, 4, *tile, dtype=BF), vmem(depth, 4, *tile),
        vmem(SLOTS * LANES, 2 * LANES, dtype=BF), vmem(SLOTS * LANES, 2 * LANES, dtype=BF),
        vmem(SLOTS * 2 * LANES, 2 * LANES, dtype=BF), vmem(LANES, LANES, dtype=BF),
        vmem(depth, 2 * LANES, LANES, dtype=BF),
        vmem(2, GROUP, 4, rows + 24, LANES), vmem(4, *tile),
        vmem(2, chips, 2, 8, LANES), vmem(chips, 2, 8, LANES),
        vmem(chips, 16, LANES, dtype=jnp.int16), vmem(chips, 16, LANES, dtype=jnp.int16),
        dma((6,)), dma((2,)), dma((2,)), dma((2, 2)), dma((2, 2)), dma((4,)), dma((4,)), dma, dma,
        dma((chips,)), dma((chips,)),
    ]
    inside = pl.BlockSpec(memory_space=pltpu.VMEM)
    anywhere = pl.BlockSpec(memory_space=pltpu.HBM)
    return pl.pallas_call(
        kernel,
        out_shape=jax.ShapeDtypeStruct((4, rows // ndep, LANES), F32),
        in_specs=[anywhere] * 6,
        out_specs=inside,
        scratch_shapes=scratch,
        compiler_params=pltpu.CompilerParams(
            collective_id=0, has_side_effects=True, vmem_limit_bytes=64 * 2 ** 20
        ),
    )(skew, frac, absorption, glow, density, temperature)


def solution(mesh):
    in_specs = (P("depth", None, "cols"), P("depth", None, "cols"), P(), P(), P(), P())
    out_specs = P(None, "depth", "cols")
    return jax.shard_map(
        on_device, mesh=mesh, in_specs=in_specs, out_specs=out_specs, check_vma=False
    )
```
